32 devices in a mesh: wide: 16 (over z, y, x), narrow: 2 (over core).
Axes of the slice: x: 2, y: 2, z: 4, core: 2. Of those that a mesh axis runs over, the one named last changes fastest.
Arguments:
- live_counts: int32 [16, 3], P('wide'), may hold values from 2 to 4, as said below
- small_in: bfloat16 [64, 5, 5, 2048], P('wide', None, None, 'narrow'), may hold values from -8 to 8
- mid_in: bfloat16 [64, 6, 6, 2048], P('wide', None, None, 'narrow'), may hold values from -8 to 8
- big_in: bfloat16 [64, 7, 7, 2048], P('wide', None, None, 'narrow'), may hold values from -8 to 8
- conv_first: bfloat16 [2048, 512], P(None, 'narrow'), may hold values from -0.125 to 0.125
- conv_middle: bfloat16 [4608, 512], P(None, 'narrow'), may hold values from -0.09375 to 0.09375
- conv_last: bfloat16 [512, 2048], P(None, 'narrow'), may hold values from -0.25 to 0.25
- gain_first: float32 [512], P('narrow'), may hold values from 0.5 to 1.5
- shift_first: float32 [512], P('narrow'), may hold values from -3 to 3
- gain_middle: float32 [512], P('narrow'), may hold values from 0.5 to 1.5
- shift_middle: float32 [512], P('narrow'), may hold values from -3 to 3
- gain_last: float32 [2048], P('narrow'), may hold values from 0.5 to 1.5
- shift_last: float32 [2048], P('narrow'), may hold values from -3 to 3
- small_cot: bfloat16 [64, 5, 5, 2048], P('wide', None, None, 'narrow'), may hold values from -6 to 6
- mid_cot: bfloat16 [64, 6, 6, 2048], P('wide', None, None, 'narrow'), may hold values from -6 to 6
- big_cot: bfloat16 [64, 7, 7, 2048], P('wide', None, None, 'narrow'), may hold values from -6 to 6
Outputs:
- small_out: bfloat16 [64, 5, 5, 2048], P('wide', None, None, 'narrow')
- mid_out: bfloat16 [64, 6, 6, 2048], P('wide', None, None, 'narrow')
- big_out: bfloat16 [64, 7, 7, 2048], P('wide', None, None, 'narrow')
- small_grad: bfloat16 [64, 5, 5, 2048], P('wide', None, None, 'narrow')
- mid_grad: bfloat16 [64, 6, 6, 2048], P('wide', None, None, 'narrow')
- big_grad: bfloat16 [64, 7, 7, 2048], P('wide', None, None, 'narrow')
- first_grad: float32 [2048, 512], P('wide', 'narrow')
- middle_grad: float32 [4608, 512], P('wide', 'narrow')
- last_grad: float32 [512, 2048], P('wide', 'narrow')
- gain_first_grad: float32 [512], P('narrow')
- shift_first_grad: float32 [512], P('narrow')
- gain_middle_grad: float32 [512], P('narrow')
- shift_middle_grad: float32 [512], P('narrow')
- gain_last_grad: float32 [2048], P('narrow')
- shift_last_grad: float32 [2048], P('narrow')
The draws below stay inside these ranges and needn't reach their ends.
Inputs may be any that keep to these rules, and one draw needn't show every extreme that they name: `live_counts`: every device has between (4 + 1) // 2 and 4 live images of each resolution, the live ones first; in every draw some device is full in all three groups and another holds (4 + 1) // 2 in all three.
All inputs are finite; a program needn't handle non-finite values.
Results may differ from the reference program's by a relative error of at most 0.02.
Values may be sent and summed in bfloat16 or wider, within the bound.
A program may use at most 128 MiB of HBM per device.

```python
import jax
import jax.numpy as jnp
from jax import lax

C = 2048
M = 512
SLOTS = 4
IMAGES = 64
N_WIDE = 16


def make_images(key, side):
    rows_all = N_WIDE * SLOTS
    key_normal = jax.random.fold_in(key, 1)
    normal_part = jax.random.normal(key_normal, (rows_all, side, side, C), jnp.float32)
    device_pos = (jnp.arange(rows_all) // SLOTS).astype(jnp.float32) / max(N_WIDE - 1, 1)
    ramp = (0.6 + 1.2 * device_pos)[:, None, None, None]
    values = ramp * normal_part
    return jnp.clip(values, -8.0, 8.0)


def draw_small_in(key, part):
    key = jax.random.fold_in(key, 11)
    return make_images(key, 5).astype(jnp.bfloat16)


def draw_mid_in(key, part):
    key = jax.random.fold_in(key, 12)
    return make_images(key, 6).astype(jnp.bfloat16)


def draw_big_in(key, part):
    key = jax.random.fold_in(key, 13)
    return make_images(key, 7).astype(jnp.bfloat16)


def draw_live_counts(key, part):
    key = jax.random.fold_in(key, 7)
    least = (SLOTS + 1) // 2
    key_counts = jax.random.fold_in(key, 1)
    key_order = jax.random.fold_in(key, 2)
    drawn = jax.random.randint(key_counts, (N_WIDE, 3), least, SLOTS + 1, jnp.int32)
    shuffled = jax.random.permutation(key_order, N_WIDE)
    device_ids = jnp.arange(N_WIDE, dtype=jnp.int32)[:, None]
    drawn = jnp.where(device_ids == shuffled[0], SLOTS, drawn)
    drawn = jnp.where(device_ids == shuffled[1], least, drawn)
    return drawn.astype(jnp.int32)


def levels(own_key, shape, cuts, low, top_value):
    def one(dim, blocks):
        heights = jax.random.uniform(jax.random.fold_in(jax.random.fold_in(own_key, 6), dim), (blocks,), jnp.float32, low / len(cuts), top_value / len(cuts))
        return jnp.repeat(jnp.exp(heights), shape[dim] // blocks).reshape((-1,) + (1,) * (len(shape) - dim - 1))

    factor_of = one(*cuts[0])
    for cut in cuts[1:]:
        factor_of = factor_of * one(*cut)
    return factor_of


def bell_draw(rng, dims, deviation, most, shards=(), kind=jnp.bfloat16):
    loudness = levels(rng, dims, shards, -0.22, 0.18) if shards else 1.0
    values = jax.random.normal(rng, dims, jnp.float32) * deviation * loudness
    return jnp.minimum(jnp.maximum(values, -most), most).astype(kind)


def setup_inputs(seed: int = 0) -> dict:
    key_of = jax.random.split(jax.random.key(seed), 17)
    live_counts = draw_live_counts(jax.random.fold_in(key_of[16], 71), 0)
    small_in = draw_small_in(jax.random.fold_in(key_of[16], 71), 0)
    mid_in = draw_mid_in(jax.random.fold_in(key_of[16], 71), 0)
    big_in = draw_big_in(jax.random.fold_in(key_of[16], 71), 0)
    conv_first = bell_draw(key_of[4], (C, M), C ** -0.5, 0.125, ((1, 2),))
    conv_middle = bell_draw(key_of[5], (9 * M, M), (9 * M) ** -0.5, 0.09375, ((1, 2),))
    conv_last = bell_draw(key_of[6], (M, C), M ** -0.5, 0.25, ((1, 2),))
    gain_first = jnp.clip(0.5 + 1.0 * jax.random.uniform(key_of[7], (M,), jnp.float32) ** levels(key_of[7], (M,), ((0, 2),), -0.2, 0.2), 0.5, 1.5)
    shift_first = bell_draw(key_of[8], (M,), 0.5, 3.0, ((0, 2),), jnp.float32)
    gain_middle = jnp.clip(0.5 + 1.0 * jax.random.uniform(key_of[9], (M,), jnp.float32) ** levels(key_of[9], (M,), ((0, 2),), -0.2, 0.2), 0.5, 1.5)
    shift_middle = bell_draw(key_of[10], (M,), 0.5, 3.0, ((0, 2),), jnp.float32)
    gain_last = jnp.clip(0.5 + 1.0 * jax.random.uniform(key_of[11], (C,), jnp.float32) ** levels(key_of[11], (C,), ((0, 2),), -0.2, 0.2), 0.5, 1.5)
    shift_last = bell_draw(key_of[12], (C,), 0.5, 3.0, ((0, 2),), jnp.float32)
    small_cot = bell_draw(key_of[13], (IMAGES, 5, 5, C), 1.0, 6.0, ((0, 16), (3, 2)))
    mid_cot = bell_draw(key_of[14], (IMAGES, 6, 6, C), 1.0, 6.0, ((0, 16), (3, 2)))
    big_cot = bell_draw(key_of[15], (IMAGES, 7, 7, C), 1.0, 6.0, ((0, 16), (3, 2)))
    return {"live_counts": live_counts, "small_in": small_in, "mid_in": mid_in, "big_in": big_in, "conv_first": conv_first, "conv_middle": conv_middle, "conv_last": conv_last, "gain_first": gain_first, "shift_first": shift_first, "gain_middle": gain_middle, "shift_middle": shift_middle, "gain_last": gain_last, "shift_last": shift_last, "small_cot": small_cot, "mid_cot": mid_cot, "big_cot": big_cot}


@jax.custom_vjp
def low(v):
    return lax.optimization_barrier(v.astype(jnp.bfloat16)).astype(jnp.float32)

@jax.custom_vjp
def low_back(v):
    return v

def low_keep(v):
    return (low(v), None)

def low_pass(kept, grad):
    return (grad,)

def back_keep(v):
    return (v, None)

def back_low(kept, grad):
    return (low(grad),)
low.defvjp(low_keep, low_pass)
low_back.defvjp(back_keep, back_low)
epsilon = 1e-05
highest = lax.Precision.HIGHEST

def smooth(values):
    return jax.nn.gelu(values, approximate=False)

def live_masks(live_counts):
    slot_ids = jnp.arange(N_WIDE * SLOTS, dtype=jnp.int32)
    owners = slot_ids // SLOTS
    places = slot_ids % SLOTS
    result = []
    for column in range(3):
        limit = jnp.take(live_counts[:, column], owners)
        result.append((places < limit).astype(jnp.float32)[:, None, None, None])
    return result

def normalize(values, masks, count, gain, shift):
    centre = sum((lax.optimization_barrier(jnp.sum(tensor * part_mask, axis=(0, 1, 2))) for tensor, part_mask in zip(values, masks))) / count
    spread = sum((lax.optimization_barrier(jnp.sum(part_mask * jnp.square(tensor - centre), axis=(0, 1, 2))) for tensor, part_mask in zip(values, masks))) / count
    scaled = lax.rsqrt(spread + epsilon)
    return [(tensor - centre) * scaled * gain + shift for tensor in values]

def forward(inputs, conv_first, conv_middle, conv_last, gains, shifts, masks):
    count = sum((jnp.sum(part_mask) * tensor.shape[1] * tensor.shape[2] for tensor, part_mask in zip(inputs, masks)))
    first = [low_back(jnp.dot(tensor.reshape(-1, C), conv_first, precision=highest).reshape(tensor.shape[:3] + (M,))) for tensor in inputs]
    hidden_one = [low(smooth(tensor)) for tensor in normalize(first, masks, count, gains[0], shifts[0])]
    kernel = conv_middle.reshape(3, 3, M, M)
    second = [low_back(lax.conv_general_dilated(tensor, kernel, (1, 1), 'SAME', dimension_numbers=('NHWC', 'HWIO', 'NHWC'), precision=highest)) for tensor in hidden_one]
    hidden_two = [low(smooth(tensor)) for tensor in normalize(second, masks, count, gains[1], shifts[1])]
    third = [low_back(jnp.dot(tensor.reshape(-1, M), conv_last, precision=highest).reshape(tensor.shape[:3] + (C,))) for tensor in hidden_two]
    branch = normalize(third, masks, count, gains[2], shifts[2])
    return tuple((part_mask * smooth(side + tensor) for side, tensor, part_mask in zip(branch, inputs, masks)))

def reference(live_counts, small_in, mid_in, big_in, conv_first, conv_middle, conv_last, gain_first, shift_first, gain_middle, shift_middle, gain_last, shift_last, small_cot, mid_cot, big_cot):
    masks = live_masks(live_counts)
    inputs = tuple((tensor.astype(jnp.float32) for tensor in (small_in, mid_in, big_in)))
    weights = (conv_first.astype(jnp.float32), conv_middle.astype(jnp.float32), conv_last.astype(jnp.float32))
    gains = (gain_first, gain_middle, gain_last)
    shifts = (shift_first, shift_middle, shift_last)

    def closed(images, first_w, middle_w, last_w, gain_set, shift_set):
        return forward(images, first_w, middle_w, last_w, gain_set, shift_set, masks)
    outputs, pullback = jax.vjp(closed, inputs, weights[0], weights[1], weights[2], gains, shifts)
    cots = tuple((tensor.astype(jnp.float32) for tensor in (small_cot, mid_cot, big_cot)))
    grad_in, grad_first, grad_middle, grad_last, grad_gains, grad_shifts = pullback(cots)
    half = jnp.bfloat16
    return (outputs[0].astype(half), outputs[1].astype(half), outputs[2].astype(half), grad_in[0].astype(half), grad_in[1].astype(half), grad_in[2].astype(half), grad_first, grad_middle, grad_last, grad_gains[0], grad_shifts[0], grad_gains[1], grad_shifts[1], grad_gains[2], grad_shifts[2])
```

```python
import functools

import jax
import jax.numpy as jnp
from jax import lax
from jax.experimental import pallas as pl
from jax.experimental.pallas import tpu as pltpu
from jax.sharding import PartitionSpec as P

MESH = pl.DeviceIdType.MESH
EPSILON = 1e-05
F32 = jnp.float32
BF16 = jnp.bfloat16
LANES = 128
CHUNK = 16
GUARD = 64


def ceil_to(value, step):
    return (value + step - 1) // step * step


class Geometry:
    def __init__(self, wide, shapes, channels, hidden, half):
        self.wide = wide
        self.slots = shapes[0][0]
        self.sides = [(shape[1], shape[2]) for shape in shapes]
        self.pixels = [height * width for height, width in self.sides]
        self.real = [count * self.slots for count in self.pixels]
        self.padded = [ceil_to(count, CHUNK) for count in self.real]
        self.starts = [sum(self.padded[:index]) for index in range(len(shapes))]
        self.rows = sum(self.padded)
        self.chunks = self.rows // CHUNK
        self.channels = channels
        self.hidden = hidden
        self.half = half
        self.wide_half = channels // 2
        self.shares = (hidden // wide, 9 * hidden // wide, channels // wide)
        bits = wide.bit_length() - 1
        self.bits = bits
        self.scattered = (
            wide >= 8 and wide == 1 << bits and all(share % CHUNK == 0 for share in self.shares)
        )


def span(start, size):
    return pl.ds(pl.multiple_of(start, size), size)


def dot(left, right):
    return lax.dot_general(left, right, (((1,), (0,)), ((), ())), preferred_element_type=F32)


def dot_turned(left, right):
    return lax.dot_general(left, right, (((1,), (1,)), ((), ())), preferred_element_type=F32)


def gelu_parts(value):
    share = 0.5 + 0.5 * lax.erf(value * 0.7071067811865476)
    slope = share + value * (jnp.exp(value * value * -0.5) * 0.3989422804014327)
    return share, slope


def block_kernel(geo, *refs):
    refs = list(refs)

    def take(count):
        taken = refs[:count]
        del refs[:count]
        return taken

    (live_counts,) = take(1)
    inputs = take(3)
    first_hbm, middle_hbm, last_hbm = take(3)
    affine_hbm = take(6)
    cots = take(3)
    outs = take(3)
    in_grads = take(3)
    weight_outs = take(3)
    affine_outs = take(6)
    raw_x, raw_cot, raw_out, raw_grad = take(3), take(3), take(3), take(3)
    conv_first, conv_middle, conv_last = take(3)
    affine = take(6)
    live, shift_masks = take(2)
    x_all, x_turned, cot_rows = take(3)
    norm_one, norm_two, norm_three = take(3)
    slope_act_one, slope_act_two = take(2)
    hidden_one, hidden_two, turned_one, turned_two = take(4)
    parts, shifted_src, shifted = take(3)
    up_three, out_rows, up_two, up_one = take(4)
    slope_three, slope_two, slope_one = take(3)
    send_two, recv_two, send_one, recv_one, send_in, recv_in = take(6)
    stat_bufs = take(6)
    totals = take(3)
    staged = [take(6) for _ in range(3)] if geo.scattered else None
    weight_stage = take(3)
    affine_stage = take(6)
    load_sem, out_sem, sib_send, sib_recv, stat_send, stat_recv = take(6)
    rs_send, rs_recv = take(2) if geo.scattered else (None, None)
    assert not refs

    wide, slots, half = geo.wide, geo.slots, geo.half
    me = lax.axis_index("wide")
    core = lax.axis_index("narrow")
    other = 1 - core

    loads = {}

    def load(name, source, target):
        loads[name] = pltpu.make_async_copy(source, target, load_sem.at[len(loads)])
        loads[name].start()

    for group in range(3):
        load(("x", group), inputs[group], raw_x[group])
    load("first", first_hbm, conv_first)
    for index in range(6):
        load(("affine", index), affine_hbm[index], affine[index])
    load("middle", middle_hbm, conv_middle)
    load("last", last_hbm, conv_last)
    for group in range(3):
        load(("cot", group), cots[group], raw_cot[group])

    barrier = pltpu.get_barrier_semaphore()

    def greet(index, carry):
        peer = lax.rem(me + 1 + index, wide)
        pl.semaphore_signal(barrier, inc=1, device_id=(peer, core), device_id_type=MESH)
        return carry

    lax.fori_loop(0, wide - 1, greet, 0)
    pl.semaphore_signal(barrier, inc=1, device_id=(me, other), device_id_type=MESH)

    local_count = 0
    for group in range(3):
        rows = geo.padded[group]
        limit = live_counts[0, group]
        local_count = local_count + limit * geo.pixels[group]
        index = lax.broadcasted_iota(jnp.int32, (rows, LANES), 0)
        image = index % slots
        mask = jnp.where((index < geo.real[group]) & (image < limit), 1.0, 0.0)
        live[geo.starts[group] : geo.starts[group] + rows, :] = mask
    count_here = jnp.full((1, LANES), local_count, jnp.int32).astype(F32)

    shift_masks[...] = jnp.ones_like(shift_masks)
    for group in range(3):
        height, width = geo.sides[group]
        start = geo.starts[group]
        line = width * slots
        for position in range(9):
            down, right = position // 3 - 1, position % 3 - 1
            if down == -1:
                shift_masks[position, start : start + line, :] = jnp.zeros((line, LANES), F32)
            if down == 1:
                low = start + (height - 1) * line
                shift_masks[position, low : low + line, :] = jnp.zeros((line, LANES), F32)
            if right:
                for row in range(height):
                    low = start + row * line + (0 if right == -1 else line - slots)
                    shift_masks[position, low : low + slots, :] = jnp.zeros((slots, LANES), F32)
    for buffer in (parts,):
        for position in range(9):
            buffer[position, 0:GUARD, :] = jnp.zeros((GUARD, half), F32)
            buffer[position, GUARD + geo.rows :, :] = jnp.zeros((GUARD, half), F32)
    shifted_src[0:GUARD, :] = jnp.zeros((GUARD, half), F32)
    shifted_src[GUARD + geo.rows :, :] = jnp.zeros((GUARD, half), F32)

    def spread(tile, width):
        return jnp.concatenate([tile] * (width // LANES), axis=1)

    def live_rows(rows, width):
        return spread(live[rows, :], width)

    def over_rows(body, init, unroll=1):
        return lax.fori_loop(
            0, geo.chunks, lambda step, carry: body(span(step * CHUNK, CHUNK), carry), init, unroll=unroll
        )

    def fold_rows(value):
        return sum(value[index * 8 : index * 8 + 8] for index in range(CHUNK // 8))

    def column_sum(value):
        return jnp.sum(value, axis=0, keepdims=True)

    to_other = {"device_id": (me, other), "device_id_type": MESH}

    def sibling(index, source, target):
        return pltpu.make_async_remote_copy(
            src_ref=source, dst_ref=target, send_sem=sib_send.at[index], recv_sem=sib_recv.at[index], **to_other
        )

    x_copies = []
    pl_wait_done = False
    for group in range(3):
        loads[("x", group)].wait()
        rows, real, start = geo.padded[group], geo.real[group], geo.starts[group]
        value = raw_x[group][...].astype(F32).reshape(real, geo.wide_half)
        if rows > real:
            value = jnp.concatenate([value, jnp.zeros((rows - real, geo.wide_half), F32)], axis=0)
        mask = spread(live[start : start + rows, :], geo.wide_half)
        place = x_all.at[core, pl.ds(start, rows)]
        place[...] = (value * mask).astype(BF16)
        if not pl_wait_done:
            pl.semaphore_wait(barrier, wide)
            pl_wait_done = True
        copy = sibling(group, place, place)
        copy.start()
        x_copies.append(copy)

    loads["first"].wait()
    norm_one[...] = dot(x_all[core], conv_first[span(core * geo.wide_half, geo.wide_half), :])
    for copy in x_copies:
        copy.wait_recv()
    norm_one[...] += dot(x_all[other], conv_first[span(other * geo.wide_half, geo.wide_half), :])

    def broadcast(round_index):
        buffer = stat_bufs[round_index]

        def push(index, carry):
            peer = lax.rem(me + 1 + index, wide)
            pltpu.make_async_remote_copy(
                src_ref=buffer.at[me],
                dst_ref=buffer.at[me],
                send_sem=stat_send.at[round_index],
                recv_sem=stat_recv.at[round_index],
                device_id=(peer, core),
                device_id_type=MESH,
            ).start()
            return carry

        lax.fori_loop(0, wide - 1, push, 0)

    def stat_wait(round_index, sem):
        view = stat_bufs[round_index].at[pl.ds(0, wide - 1)]
        pltpu.make_async_copy(view, view, sem.at[round_index]).wait()

    def send_moments(round_index, values, width):
        def add(rows, carry):
            return carry + fold_rows(values[rows, :] * live_rows(rows, width))

        total = column_sum(over_rows(add, jnp.zeros((8, width), F32)))
        centre = total / spread(count_here, width)

        def add_square(rows, carry):
            gap = (values[rows, :] - centre) * live_rows(rows, width)
            return carry + fold_rows(gap * gap)

        squares = column_sum(over_rows(add_square, jnp.zeros((8, width), F32)))
        buffer = stat_bufs[round_index]
        buffer[me, 0:1, :] = total
        buffer[me, 1:2, :] = squares
        if round_index == 0:
            buffer[me, 2:3, :] = spread(count_here, width)
        broadcast(round_index)

    def counts(width):
        return [spread(stat_bufs[0][index, 2:3, 0:LANES], width) for index in range(wide)]

    def get_moments(round_index, width):
        stat_wait(round_index, stat_recv)
        buffer = stat_bufs[round_index]
        each = counts(width)
        total_count = sum(each)
        centre = sum(buffer[index, 0:1, :] for index in range(wide)) / total_count
        squares = jnp.zeros((1, width), F32)
        for index in range(wide):
            gap = buffer[index, 0:1, :] / each[index] - centre
            squares = squares + (buffer[index, 1:2, :] + each[index] * gap * gap)
        return centre, lax.rsqrt(squares / total_count + EPSILON), 1.0 / total_count

    def send_sums(round_index, first, second):
        buffer = stat_bufs[round_index]
        buffer[me, 0:1, :] = column_sum(first)
        buffer[me, 1:2, :] = column_sum(second)
        broadcast(round_index)

    def get_sums(round_index):
        stat_wait(round_index, stat_recv)
        buffer = stat_bufs[round_index]
        total = sum(buffer[index] for index in range(wide))
        return total[0:1, :], total[1:2, :]

    def activate(values, slope_act, hidden, centre, scale, gain, shift):
        def step(rows, carry):
            mask = live_rows(rows, half)
            normed = (values[rows, :] - centre) * scale
            values[rows, :] = normed
            act = normed * gain + shift
            share, slope = gelu_parts(act)
            hidden[core, rows, :] = (act * share * mask).astype(BF16)
            slope_act[rows, :] = slope * mask
            return carry

        over_rows(step, 0)

    def gather_shifted(source, position, group):
        width = geo.sides[group][1]
        shift = slots * ((position // 3 - 1) * width + position % 3 - 1)
        low = GUARD + geo.starts[group] + shift
        return source[low : low + geo.padded[group], :]

    def fold_parts(pick):
        results = []
        for group in range(3):
            start, rows = geo.starts[group], geo.padded[group]
            total = None
            for position in range(9):
                value = gather_shifted(parts.at[pick(position)], position, group)
                if position != 4:
                    value = value * spread(shift_masks[position, start : start + rows, :], half)
                total = value if total is None else total + value
            results.append(total)
        return results

    send_moments(0, norm_one, half)
    for index in range(2):
        x_turned[index * geo.wide_half : (index + 1) * geo.wide_half, :] = x_all[index].T
    for index in range(6):
        loads[("affine", index)].wait()
    gain_one, shift_one, gain_two, shift_two, gain_three, shift_three = (ref[...] for ref in affine)
    centre_one, scale_one, inverse = get_moments(0, half)
    activate(norm_one, slope_act_one, hidden_one, centre_one, scale_one, gain_one, shift_one)
    copy_one = sibling(3, hidden_one.at[core], hidden_one.at[core])
    copy_one.start()
    loads["middle"].wait()
    copy_one.wait_recv()

    whole = slice(GUARD, GUARD + geo.rows)
    for position in range(9):
        low = position * geo.hidden
        parts[position, whole, :] = dot(hidden_one[0], conv_middle[low : low + half, :]) + dot(
            hidden_one[1], conv_middle[low + half : low + geo.hidden, :]
        )
    for group, value in enumerate(fold_parts(lambda position: position)):
        norm_two[geo.starts[group] : geo.starts[group] + geo.padded[group], :] = value
    send_moments(1, norm_two, half)
    for index in range(2):
        turned_one[index * half : (index + 1) * half, :] = hidden_one[index].T
    for group in range(3):
        loads[("cot", group)].wait()
        rows, real, start = geo.padded[group], geo.real[group], geo.starts[group]
        value = raw_cot[group][...].astype(F32).reshape(real, geo.wide_half)
        if rows > real:
            value = jnp.concatenate([value, jnp.zeros((rows - real, geo.wide_half), F32)], axis=0)
        cot_rows[start : start + rows, :] = value * spread(live[start : start + rows, :], geo.wide_half)
    centre_two, scale_two, _ = get_moments(1, half)
    activate(norm_two, slope_act_two, hidden_two, centre_two, scale_two, gain_two, shift_two)
    copy_two = sibling(4, hidden_two.at[core], hidden_two.at[core])
    copy_two.start()
    loads["last"].wait()
    copy_two.wait_recv()
    norm_three[...] = dot(hidden_two[0], conv_last[0:half, :]) + dot(hidden_two[1], conv_last[half:, :])
    send_moments(2, norm_three, geo.wide_half)
    for index in range(2):
        turned_two[index * half : (index + 1) * half, :] = hidden_two[index].T
    centre_three, scale_three, inverse_wide = get_moments(2, geo.wide_half)

    def finish(rows, carry):
        grad_sum, cross_sum = carry
        normed = (norm_three[rows, :] - centre_three) * scale_three
        norm_three[rows, :] = normed
        before = normed * gain_three + shift_three + x_all[core, rows, :].astype(F32)
        share, slope = gelu_parts(before)
        out_rows[rows, :] = before * share * live_rows(rows, geo.wide_half)
        up = cot_rows[rows, :] * slope
        up_three[rows, :] = up
        return grad_sum + fold_rows(up), cross_sum + fold_rows(up * normed)

    zero_wide = jnp.zeros((8, geo.wide_half), F32)
    send_sums(3, *over_rows(finish, (zero_wide, zero_wide)))

    stores = []

    def store(source, target):
        copy = pltpu.make_async_copy(source, target, out_sem.at[len(stores)])
        copy.start()
        stores.append(copy)

    for group in range(3):
        start, real = geo.starts[group], geo.real[group]
        value = out_rows[start : start + real, :].reshape(geo.pixels[group], slots, geo.wide_half)
        raw_out[group][...] = value.astype(BF16)
        store(raw_out[group], outs[group])

    def slopes(up, normed, target, scale, gain, sums, inverse_count, width, plain=None):
        grad_total, cross_total = sums
        factor = gain * scale
        grad_mean, cross_mean = grad_total * inverse_count, cross_total * inverse_count

        def step(rows, carry):
            value = live_rows(rows, width) * (
                factor * (up[rows, :] - grad_mean - normed[rows, :] * cross_mean)
            )
            target[rows, :] = value.astype(BF16)
            if plain is not None:
                plain[pl.ds(pl.multiple_of(GUARD + rows.start, CHUNK), CHUNK), :] = value
            return carry

        over_rows(step, 0)

    def give_affine(index, sums):
        affine_stage[2 * index][...] = sums[1]
        affine_stage[2 * index + 1][...] = sums[0]
        for place in (2 * index, 2 * index + 1):
            store(affine_stage[place], affine_outs[place])

    def weigh(stage):
        if stage == 0:
            return 1 + core
        if stage == 1:
            return 2 - core
        return 1 << stage

    def owner(slot):
        place = me
        for stage in range(geo.bits):
            chosen = (slot // (1 << (geo.bits - 1 - stage))) % 2
            weight = weigh(stage)
            mine = (me // weight) % 2
            place = place + chosen * (1 - 2 * mine) * weight
        return place

    def owned(which, slot):
        share = geo.shares[which]
        return totals[which][pl.ds(pl.multiple_of(owner(slot) * share, CHUNK), share), :]

    def over_slots(low, high, body):
        lax.fori_loop(low, high, lambda slot, carry: (body(slot), carry)[1], 0)

    def rs_copy(which, stage, source, target, slot):
        return pltpu.make_async_remote_copy(
            src_ref=source,
            dst_ref=target,
            send_sem=rs_send.at[which, stage],
            recv_sem=rs_recv.at[which, stage],
            device_id=(owner(slot), core),
            device_id_type=MESH,
        )

    def rs_first(which):
        if not geo.scattered:
            return
        send_a, recv_a = staged[which][0:2]
        many = wide // 2

        def fill(slot):
            send_a[slot - many] = owned(which, slot).astype(BF16)

        over_slots(many, wide, fill)
        rs_copy(which, 0, send_a, recv_a, many).start()

    def rs_second(which):
        if not geo.scattered:
            return
        send_a, recv_a, send_b, recv_b = staged[which][0:4]
        rs_copy(which, 0, send_a, recv_a, wide // 2).wait_recv()
        many = wide // 4

        def fill(slot):
            send_b[slot - many] = (owned(which, slot) + recv_a[slot].astype(F32)).astype(BF16)

        over_slots(many, 2 * many, fill)
        rs_copy(which, 1, send_b, recv_b, many).start()

    def rs_third(which):
        if not geo.scattered:
            return
        _, recv_a, send_b, recv_b, send_c, recv_c = staged[which]
        rs_copy(which, 1, send_b, recv_b, wide // 4).wait_recv()

        def fill(slot):
            send_c[slot - 1] = (
                owned(which, slot) + recv_a[slot].astype(F32) + recv_b[slot].astype(F32)
            ).astype(BF16)
            rs_copy(which, 2, send_c.at[slot - 1], recv_c.at[slot - 1], slot).start()

        over_slots(1, wide // 4, fill)

    def rs_last(which):
        if not geo.scattered:
            store(totals[which], weight_outs[which])
            return
        _, recv_a, _, recv_b, _, recv_c = staged[which]
        pltpu.make_async_copy(recv_c, recv_c, rs_recv.at[which, 2]).wait()
        value = owned(which, 0) + recv_a[0].astype(F32) + recv_b[0].astype(F32)
        for index in range(wide // 4 - 1):
            value = value + recv_c[index].astype(F32)
        weight_stage[which][...] = value
        store(weight_stage[which], weight_outs[which])

    def rs_drain(which):
        if not geo.scattered:
            return
        for stage in range(3):
            source = staged[which][2 * stage]
            pltpu.make_async_copy(source, source, rs_send.at[which, stage]).wait()

    sums_three = get_sums(3)
    slopes(
        up_three, norm_three, slope_three, scale_three, gain_three, sums_three, inverse_wide, geo.wide_half
    )
    send_two[...] = dot_turned(slope_three[...], conv_last[span(other * half, half), :]).astype(BF16)
    copy_back_two = sibling(5, send_two, recv_two)
    copy_back_two.start()
    totals[0][...] = dot(turned_two[...], slope_three[...])
    rs_first(0)
    up_two[...] = dot_turned(slope_three[...], conv_last[span(core * half, half), :])
    give_affine(2, sums_three)
    copy_back_two.wait_recv()

    def back_sums(up, received, slope_act, normed):
        def step(rows, carry):
            value = (up[rows, :] + received[rows, :].astype(F32)) * slope_act[rows, :]
            up[rows, :] = value
            return carry[0] + fold_rows(value), carry[1] + fold_rows(value * normed[rows, :])

        zero = jnp.zeros((8, half), F32)
        return over_rows(step, (zero, zero))

    send_sums(4, *back_sums(up_two, recv_two, slope_act_two, norm_two))
    sums_two = get_sums(4)
    slopes(up_two, norm_two, slope_two, scale_two, gain_two, sums_two, inverse, half, shifted_src)

    def back_parts(low):
        for position in range(9):
            rows = pl.ds(pl.multiple_of(position * geo.hidden + low, half), half)
            parts[position, whole, :] = dot_turned(slope_two[...], conv_middle[rows, :])
        return fold_parts(lambda position: 8 - position)

    for group, value in enumerate(back_parts(other * half)):
        send_one[geo.starts[group] : geo.starts[group] + geo.padded[group], :] = value.astype(BF16)
    copy_back_one = sibling(6, send_one, recv_one)
    copy_back_one.start()
    for position in range(9):
        flipped = 8 - position
        for group in range(3):
            start, rows = geo.starts[group], geo.padded[group]
            value = gather_shifted(shifted_src, flipped, group)
            if position != 4:
                value = value * spread(shift_masks[flipped, start : start + rows, :], half)
            shifted[start : start + rows, :] = value.astype(BF16)
        totals[1][position * geo.hidden : (position + 1) * geo.hidden, :] = dot(
            turned_one[...], shifted[...]
        )
    rs_first(1)
    for group, value in enumerate(back_parts(core * half)):
        up_one[geo.starts[group] : geo.starts[group] + geo.padded[group], :] = value
    give_affine(1, sums_two)
    rs_second(0)
    copy_back_one.wait_recv()

    send_sums(5, *back_sums(up_one, recv_one, slope_act_one, norm_one))
    rs_third(0)
    sums_one = get_sums(5)
    slopes(up_one, norm_one, slope_one, scale_one, gain_one, sums_one, inverse, half)
    send_in[...] = dot_turned(
        slope_one[...], conv_first[span(other * geo.wide_half, geo.wide_half), :]
    ).astype(BF16)
    copy_in = sibling(7, send_in, recv_in)
    copy_in.start()
    totals[2][...] = dot(x_turned[...], slope_one[...])
    rs_first(2)
    rs_second(1)
    up_three[...] += dot_turned(slope_one[...], conv_first[span(core * geo.wide_half, geo.wide_half), :])
    give_affine(0, sums_one)
    copy_in.wait_recv()
    for group in range(3):
        start, real, rows = geo.starts[group], geo.real[group], geo.padded[group]
        value = up_three[start : start + rows, :] + recv_in[start : start + rows, :].astype(F32)
        value = value[0:real, :].reshape(geo.pixels[group], slots, geo.wide_half)
        raw_grad[group][...] = value.astype(BF16)
        store(raw_grad[group], in_grads[group])
    rs_last(0)
    rs_third(1)
    rs_second(2)
    rs_third(2)
    rs_last(1)
    rs_last(2)

    for copy in (*x_copies, copy_one, copy_two, copy_back_two, copy_back_one, copy_in):
        copy.wait_send()
    for round_index in range(6):
        stat_wait(round_index, stat_send)
    for which in range(3):
        rs_drain(which)
    for copy in stores:
        copy.wait()


def run_block(
    wide,
    live_counts,
    small_in,
    mid_in,
    big_in,
    conv_first,
    conv_middle,
    conv_last,
    gain_first,
    shift_first,
    gain_middle,
    shift_middle,
    gain_last,
    shift_last,
    small_cot,
    mid_cot,
    big_cot,
):
    maps = (small_in, mid_in, big_in)
    cots = (small_cot, mid_cot, big_cot)
    channels = 2 * small_in.shape[3]
    hidden, half = conv_last.shape[0], conv_first.shape[1]
    geo = Geometry(wide, [tensor.shape for tensor in maps], channels, hidden, half)
    across = geo.wide_half

    def as_rows(tensor):
        count, height, width, depth = tensor.shape
        return jnp.transpose(tensor, (1, 2, 0, 3)).reshape(height * width, count, depth)

    def as_maps(rows, like):
        count, height, width, depth = like.shape
        return jnp.transpose(rows.reshape(height, width, count, depth), (2, 0, 1, 3))

    affine = [
        vector.reshape(1, -1)
        for vector in (gain_first, shift_first, gain_middle, shift_middle, gain_last, shift_last)
    ]
    operands = [
        live_counts,
        *[as_rows(tensor) for tensor in maps],
        conv_first,
        conv_middle,
        conv_last,
        *affine,
        *[as_rows(tensor) for tensor in cots],
    ]
    raw_shapes = [(count, geo.slots, across) for count in geo.pixels]
    weight_shapes = [(hidden, across), (9 * hidden, half), (channels, half)]
    share_shapes = [
        (share, shape[1]) if geo.scattered else shape
        for share, shape in zip(geo.shares, weight_shapes)
    ]
    out_shapes = [jax.ShapeDtypeStruct(shape, BF16) for shape in raw_shapes * 2]
    out_shapes += [jax.ShapeDtypeStruct(shape, F32) for shape in share_shapes]
    out_shapes += [jax.ShapeDtypeStruct(vector.shape, F32) for vector in affine]

    def vmem(dtype, *shape):
        return pltpu.VMEM(shape, dtype)

    rows, guarded = geo.rows, geo.rows + 2 * GUARD
    scratch = [vmem(BF16, *shape) for shape in raw_shapes * 4]
    scratch += [vmem(BF16, *tensor.shape) for tensor in (conv_first, conv_middle, conv_last)]
    scratch += [vmem(F32, *vector.shape) for vector in affine]
    scratch += [vmem(F32, rows, LANES), vmem(F32, 9, rows, LANES)]
    scratch += [vmem(BF16, 2, rows, across), vmem(BF16, channels, rows), vmem(F32, rows, across)]
    scratch += [vmem(F32, rows, half), vmem(F32, rows, half), vmem(F32, rows, across)]
    scratch += [vmem(F32, rows, half)] * 2
    scratch += [vmem(BF16, 2, rows, half)] * 2 + [vmem(BF16, hidden, rows)] * 2
    scratch += [vmem(F32, 9, guarded, half), vmem(F32, guarded, half), vmem(BF16, rows, half)]
    scratch += [vmem(F32, rows, across)] * 2 + [vmem(F32, rows, half)] * 2
    scratch += [vmem(BF16, rows, across), vmem(BF16, rows, half), vmem(BF16, rows, half)]
    scratch += [vmem(BF16, rows, half)] * 4 + [vmem(BF16, rows, across)] * 2
    scratch += [
        vmem(F32, wide, 3, half),
        vmem(F32, wide, 2, half),
        vmem(F32, wide, 2, across),
        vmem(F32, wide, 2, across),
        vmem(F32, wide, 2, half),
        vmem(F32, wide, 2, half),
    ]
    scratch += [vmem(F32, *shape) for shape in weight_shapes]
    if geo.scattered:
        for share, shape in zip(geo.shares, weight_shapes):
            for many in (wide // 2, wide // 4, wide // 4 - 1):
                scratch += [vmem(BF16, many, share, shape[1])] * 2
    scratch += [vmem(F32, *shape) for shape in (share_shapes if geo.scattered else [(8, LANES)] * 3)]
    scratch += [vmem(F32, *vector.shape) for vector in affine]
    dma = pltpu.SemaphoreType.DMA
    scratch += [dma((18,)), dma((15,)), dma((8,)), dma((8,)), dma((6,)), dma((6,))]
    if geo.scattered:
        scratch += [dma((3, 3)), dma((3, 3))]

    anywhere = pl.BlockSpec(memory_space=pl.ANY)
    results = pl.pallas_call(
        functools.partial(block_kernel, geo),
        out_shape=out_shapes,
        in_specs=[pl.BlockSpec(memory_space=pltpu.SMEM)] + [anywhere] * (len(operands) - 1),
        out_specs=[anywhere] * len(out_shapes),
        scratch_shapes=scratch,
        compiler_params=pltpu.CompilerParams(
            collective_id=0, has_side_effects=True, vmem_limit_bytes=60 * 2**20
        ),
    )(*operands)
    images = [as_maps(rows, like) for rows, like in zip(results[0:6], maps * 2)]
    last_grad, middle_grad, first_grad = results[6:9]
    if not geo.scattered:
        first_grad, middle_grad, last_grad = (
            lax.psum_scatter(grad, "wide", scatter_dimension=0, tiled=True)
            for grad in (first_grad, middle_grad, last_grad)
        )
    vectors = [vector.reshape(-1) for vector in results[9:15]]
    return (*images, first_grad, middle_grad, last_grad, *vectors)


def solution(mesh):
    images = P("wide", None, None, "narrow")
    columns = P(None, "narrow")
    vector = P("narrow")
    return jax.shard_map(
        functools.partial(run_block, mesh.shape["wide"]),
        mesh=mesh,
        in_specs=(P("wide", None),) + (images,) * 3 + (columns,) * 3 + (vector,) * 6 + (images,) * 3,
        out_specs=(images,) * 6 + (P("wide", "narrow"),) * 3 + (vector,) * 6,
        check_vma=False,
    )
```

```python
import functools

import jax
import jax.numpy as jnp
from jax import lax
from jax.experimental import pallas as pl
from jax.experimental.pallas import tpu as pltpu
from jax.sharding import PartitionSpec as P

MESH = pl.DeviceIdType.MESH
EPSILON = 1e-05
F32 = jnp.float32
BF16 = jnp.bfloat16
LANES = 128
CHUNK = 16
GUARD = 64


def ceil_to(value, step):
    return (value + step - 1) // step * step


class Geometry:
    def __init__(self, wide, shapes, channels, hidden, half):
        self.wide = wide
        self.slots = shapes[0][0]
        self.sides = [(shape[1], shape[2]) for shape in shapes]
        self.pixels = [height * width for height, width in self.sides]
        self.real = [count * self.slots for count in self.pixels]
        self.padded = [ceil_to(count, CHUNK) for count in self.real]
        self.starts = [sum(self.padded[:index]) for index in range(len(shapes))]
        self.rows = sum(self.padded)
        self.chunks = self.rows // CHUNK
        self.channels = channels
        self.hidden = hidden
        self.half = half
        self.wide_half = channels // 2
        self.shares = (hidden // wide, 9 * hidden // wide, channels // wide)
        bits = wide.bit_length() - 1
        self.bits = bits
        self.scattered = (
            wide >= 8
            and wide == 1 << bits
            and all(share % CHUNK == 0 for share in self.shares)
            and self.shares[2] % LANES == 0
            and self.wide_half % self.shares[2] == 0
        )


def span(start, size):
    return pl.ds(pl.multiple_of(start, size), size)


def dot(left, right):
    return lax.dot_general(left, right, (((1,), (0,)), ((), ())), preferred_element_type=F32)


def dot_turned(left, right):
    return lax.dot_general(left, right, (((1,), (1,)), ((), ())), preferred_element_type=F32)


def gelu_parts(value):
    share = 0.5 + 0.5 * lax.erf(value * 0.7071067811865476)
    slope = share + value * (jnp.exp(value * value * -0.5) * 0.3989422804014327)
    return share, slope


def block_kernel(geo, *refs):
    refs = list(refs)

    def take(count):
        taken = refs[:count]
        del refs[:count]
        return taken

    (live_counts,) = take(1)
    inputs = take(3)
    first_hbm, middle_hbm, last_hbm = take(3)
    affine_hbm = take(6)
    cots = take(3)
    outs = take(3)
    in_grads = take(3)
    weight_outs = take(3)
    affine_outs = take(6)
    raw_x, raw_cot, raw_out, raw_grad = take(3), take(3), take(3), take(3)
    conv_first, conv_middle, conv_last = take(3)
    affine = take(6)
    live, shift_masks = take(2)
    x_all, x_kept, x_given, cot_rows = take(4)
    norm_one, norm_two, norm_three = take(3)
    slope_act_one, slope_act_two = take(2)
    hidden_one, hidden_two, turned_one, turned_two = take(4)
    parts, shifted_src, shifted = take(3)
    up_three, out_rows, up_two, up_one = take(4)
    slope_three, slope_two, slope_one = take(3)
    send_two, recv_two, send_one, recv_one, send_in, recv_in = take(6)
    stat_bufs = take(6)
    totals = take(3)
    if geo.scattered:
        norm_one_half, norm_two_half, up_two_half, up_one_half, pair_slope = take(5)
        pair_live, pair_norm_one, pair_norm_two, pair_up_two, pair_up_one = take(5)
        pair_turned, pair_x, pair_src, live_half = take(4)
        send_a, recv_a = take(2)
        staged = [take(4) for _ in range(3)]
    weight_stage = take(3)
    affine_stage = take(6)
    load_sem, out_sem, sib_send, sib_recv, stat_send, stat_recv = take(6)
    if geo.scattered:
        rs_send, rs_recv, pair_send, pair_recv = take(4)
    assert not refs

    wide, slots, half = geo.wide, geo.slots, geo.half
    me = lax.axis_index("wide")
    core = lax.axis_index("narrow")
    other = 1 - core

    pending = {}

    def settle(*keys):
        for key in keys:
            pending.pop(key)()

    def settle_all():
        settle(*list(pending))

    load_count = iter(range(18))

    def load(name, source, target):
        copy = pltpu.make_async_copy(source, target, load_sem.at[next(load_count)])
        copy.start()
        pending[name] = copy.wait

    for group in range(3):
        load(("x", group), inputs[group], raw_x[group])
    load("first", first_hbm, conv_first)
    for index in range(6):
        load(("affine", index), affine_hbm[index], affine[index])
    load("middle", middle_hbm, conv_middle)
    load("last", last_hbm, conv_last)
    for group in range(3):
        load(("cot", group), cots[group], raw_cot[group])

    barrier = pltpu.get_barrier_semaphore()

    def greet(index, carry):
        peer = lax.rem(me + 1 + index, wide)
        pl.semaphore_signal(barrier, inc=1, device_id=(peer, core), device_id_type=MESH)
        return carry

    lax.fori_loop(0, wide - 1, greet, 0)
    pl.semaphore_signal(barrier, inc=1, device_id=(me, other), device_id_type=MESH)

    local_count = 0
    for group in range(3):
        rows = geo.padded[group]
        limit = live_counts[0, group]
        local_count = local_count + limit * geo.pixels[group]
        index = lax.broadcasted_iota(jnp.int32, (rows, LANES), 0)
        image = index % slots
        mask = jnp.where((index < geo.real[group]) & (image < limit), 1.0, 0.0)
        live[geo.starts[group] : geo.starts[group] + rows, :] = mask
        if geo.scattered:
            live_half[geo.starts[group] : geo.starts[group] + rows, :] = mask.astype(BF16)
    count_here = jnp.full((1, LANES), local_count, jnp.int32).astype(F32)

    shift_masks[...] = jnp.ones_like(shift_masks)
    for group in range(3):
        height, width = geo.sides[group]
        start = geo.starts[group]
        line = width * slots
        for position in range(9):
            down, right = position // 3 - 1, position % 3 - 1
            if down == -1:
                shift_masks[position, start : start + line, :] = jnp.zeros((line, LANES), F32)
            if down == 1:
                low = start + (height - 1) * line
                shift_masks[position, low : low + line, :] = jnp.zeros((line, LANES), F32)
            if right:
                for row in range(height):
                    low = start + row * line + (0 if right == -1 else line - slots)
                    shift_masks[position, low : low + slots, :] = jnp.zeros((slots, LANES), F32)
    for buffer in (parts,):
        for position in range(9):
            buffer[position, 0:GUARD, :] = jnp.zeros((GUARD, half), F32)
            buffer[position, GUARD + geo.rows :, :] = jnp.zeros((GUARD, half), F32)
    for buffer in (shifted_src, pair_src) if geo.scattered else (shifted_src,):
        buffer[0:GUARD, :] = jnp.zeros((GUARD, half), F32)
        buffer[GUARD + geo.rows :, :] = jnp.zeros((GUARD, half), F32)

    def spread(tile, width):
        return jnp.concatenate([tile] * (width // LANES), axis=1)

    def live_rows(rows, width):
        return spread(live[rows, :], width)

    def over_rows(body, init, unroll=1):
        return lax.fori_loop(
            0, geo.chunks, lambda step, carry: body(span(step * CHUNK, CHUNK), carry), init, unroll=unroll
        )

    def fold_rows(value):
        return sum(value[index * 8 : index * 8 + 8] for index in range(CHUNK // 8))

    def column_sum(value):
        return jnp.sum(value, axis=0, keepdims=True)

    def weigh(stage):
        if stage == 0:
            return 1 + core
        if stage == 1:
            return 2 - core
        return 1 << stage

    def owner(slot):
        place = me
        for stage in range(geo.bits):
            chosen = (slot // (1 << (geo.bits - 1 - stage))) % 2
            weight = weigh(stage)
            mine = (me // weight) % 2
            place = place + chosen * (1 - 2 * mine) * weight
        return place

    def over_slots(low, high, body):
        lax.fori_loop(low, high, lambda slot, carry: (body(slot), carry)[1], 0)

    def to_pair(name, index, source, target):
        if not geo.scattered:
            return
        copy = pltpu.make_async_remote_copy(
            src_ref=source,
            dst_ref=target,
            send_sem=pair_send.at[index],
            recv_sem=pair_recv.at[index],
            device_id=(owner(wide // 2), core),
            device_id_type=MESH,
        )
        copy.start()
        pending["pair", name] = copy.wait_recv
        pending["pair sent", name] = copy.wait_send

    to_other = {"device_id": (me, other), "device_id_type": MESH}

    def exchange(name, index, source, target):
        copy = pltpu.make_async_remote_copy(
            src_ref=source, dst_ref=target, send_sem=sib_send.at[index], recv_sem=sib_recv.at[index], **to_other
        )
        copy.start()
        pending[name] = copy.wait_recv
        pending[name, "sent"] = copy.wait_send

    greeted = False
    for group in range(3):
        settle(("x", group))
        rows, real, start = geo.padded[group], geo.real[group], geo.starts[group]
        value = raw_x[group][...].astype(F32).reshape(real, geo.wide_half)
        if rows > real:
            value = jnp.concatenate([value, jnp.zeros((rows - real, geo.wide_half), F32)], axis=0)
        mask = spread(live[start : start + rows, :], geo.wide_half)
        place = x_all.at[core, pl.ds(start, rows)]
        place[...] = (value * mask).astype(BF16)
        if not greeted:
            pl.semaphore_wait(barrier, wide)
            greeted = True
        exchange(("x other", group), group, place, place)

    settle("first")
    norm_one[...] = dot(x_all[core], conv_first[span(core * geo.wide_half, geo.wide_half), :])
    settle(*(("x other", group) for group in range(3)))
    norm_one[...] += dot(x_all[other], conv_first[span(other * geo.wide_half, geo.wide_half), :])

    def broadcast(round_index):
        buffer = stat_bufs[round_index]

        def push(index, carry):
            peer = lax.rem(me + 1 + index, wide)
            pltpu.make_async_remote_copy(
                src_ref=buffer.at[me],
                dst_ref=buffer.at[me],
                send_sem=stat_send.at[round_index],
                recv_sem=stat_recv.at[round_index],
                device_id=(peer, core),
                device_id_type=MESH,
            ).start()
            return carry

        lax.fori_loop(0, wide - 1, push, 0)
        view = buffer.at[pl.ds(0, wide - 1)]
        pending["stat", round_index] = pltpu.make_async_copy(view, view, stat_recv.at[round_index]).wait
        pending["stat sent", round_index] = pltpu.make_async_copy(view, view, stat_send.at[round_index]).wait

    def send_moments(round_index, values, width):
        def add(rows, carry):
            return carry + fold_rows(values[rows, :] * live_rows(rows, width))

        total = column_sum(over_rows(add, jnp.zeros((8, width), F32)))
        centre = total / spread(count_here, width)

        def add_square(rows, carry):
            gap = (values[rows, :] - centre) * live_rows(rows, width)
            return carry + fold_rows(gap * gap)

        squares = column_sum(over_rows(add_square, jnp.zeros((8, width), F32)))
        buffer = stat_bufs[round_index]
        buffer[me, 0:1, :] = total
        buffer[me, 1:2, :] = squares
        if round_index == 0:
            buffer[me, 2:3, :] = spread(count_here, width)
        broadcast(round_index)

    def counts(width):
        return [spread(stat_bufs[0][index, 2:3, 0:LANES], width) for index in range(wide)]

    def get_moments(round_index, width):
        settle(("stat", round_index))
        buffer = stat_bufs[round_index]
        each = counts(width)
        total_count = sum(each)
        centre = sum(buffer[index, 0:1, :] for index in range(wide)) / total_count
        squares = jnp.zeros((1, width), F32)
        for index in range(wide):
            gap = buffer[index, 0:1, :] / each[index] - centre
            squares = squares + (buffer[index, 1:2, :] + each[index] * gap * gap)
        return centre, lax.rsqrt(squares / total_count + EPSILON), 1.0 / total_count

    def send_sums(round_index, first, second):
        buffer = stat_bufs[round_index]
        buffer[me, 0:1, :] = column_sum(first)
        buffer[me, 1:2, :] = column_sum(second)
        broadcast(round_index)

    def get_sums(round_index):
        settle(("stat", round_index))
        buffer = stat_bufs[round_index]
        total = sum(buffer[index] for index in range(wide))
        return total[0:1, :], total[1:2, :]

    def activate(values, halved, slope_act, hidden, centre, scale, gain, shift):
        def step(rows, carry):
            mask = live_rows(rows, half)
            normed = (values[rows, :] - centre) * scale
            values[rows, :] = normed
            if halved is not None:
                halved[rows, :] = normed.astype(BF16)
            act = normed * gain + shift
            share, slope = gelu_parts(act)
            hidden[core, rows, :] = (act * share * mask).astype(BF16)
            slope_act[rows, :] = slope * mask
            return carry

        over_rows(step, 0)

    def gather_shifted(source, position, group):
        width = geo.sides[group][1]
        shift = slots * ((position // 3 - 1) * width + position % 3 - 1)
        low = GUARD + geo.starts[group] + shift
        return source[low : low + geo.padded[group], :]

    def fold_parts(pick):
        results = []
        for group in range(3):
            start, rows = geo.starts[group], geo.padded[group]
            total = None
            for position in range(9):
                value = gather_shifted(parts.at[pick(position)], position, group)
                if position != 4:
                    value = value * spread(shift_masks[position, start : start + rows, :], half)
                total = value if total is None else total + value
            results.append(total)
        return results

    send_moments(0, norm_one, half)
    if geo.scattered:
        share = geo.shares[2]
        per_half = geo.wide_half // share

        def turn(place, slot, target):
            low = pl.multiple_of((place % per_half) * share, share)
            target[slot] = x_all[place // per_half, :, pl.ds(low, share)].T

        many, part = wide // 2, wide // 4
        over_slots(many, many + part, lambda slot: turn(owner(slot), slot - many, x_given))
        low, high = pl.ds(0, part), pl.ds(part, part)
        to_pair("x low", 1, x_given.at[low], pair_x.at[low])
        to_pair("live", 0, live_half, pair_live)
        over_slots(many + part, wide, lambda slot: turn(owner(slot), slot - many, x_given))
        over_slots(0, many, lambda slot: turn(owner(slot), slot, x_kept))
    else:
        for index in range(2):
            x_kept[index * geo.wide_half : (index + 1) * geo.wide_half, :] = x_all[index].T
    for index in range(6):
        settle(("affine", index))
    gain_one, shift_one, gain_two, shift_two, gain_three, shift_three = (ref[...] for ref in affine)
    centre_one, scale_one, inverse = get_moments(0, half)
    half_one, half_two = (norm_one_half, norm_two_half) if geo.scattered else (None, None)
    activate(norm_one, half_one, slope_act_one, hidden_one, centre_one, scale_one, gain_one, shift_one)
    exchange("hidden one", 3, hidden_one.at[core], hidden_one.at[core])
    settle("middle", "hidden one")

    whole = slice(GUARD, GUARD + geo.rows)
    for position in range(9):
        low = position * geo.hidden
        parts[position, whole, :] = dot(hidden_one[0], conv_middle[low : low + half, :]) + dot(
            hidden_one[1], conv_middle[low + half : low + geo.hidden, :]
        )
    for group, value in enumerate(fold_parts(lambda position: position)):
        norm_two[geo.starts[group] : geo.starts[group] + geo.padded[group], :] = value
    send_moments(1, norm_two, half)
    if geo.scattered:
        to_pair("x high", 7, x_given.at[high], pair_x.at[high])
    for index in range(2):
        turned_one[index * half : (index + 1) * half, :] = hidden_one[index].T
    for group in range(3):
        settle(("cot", group))
        rows, real, start = geo.padded[group], geo.real[group], geo.starts[group]
        value = raw_cot[group][...].astype(F32).reshape(real, geo.wide_half)
        if rows > real:
            value = jnp.concatenate([value, jnp.zeros((rows - real, geo.wide_half), F32)], axis=0)
        cot_rows[start : start + rows, :] = value * spread(live[start : start + rows, :], geo.wide_half)
    centre_two, scale_two, _ = get_moments(1, half)
    activate(norm_two, half_two, slope_act_two, hidden_two, centre_two, scale_two, gain_two, shift_two)
    exchange("hidden two", 4, hidden_two.at[core], hidden_two.at[core])
    settle("last", "hidden two")
    norm_three[...] = dot(hidden_two[0], conv_last[0:half, :]) + dot(hidden_two[1], conv_last[half:, :])
    send_moments(2, norm_three, geo.wide_half)
    if geo.scattered:
        to_pair("turned", 3, turned_one, pair_turned)
    for index in range(2):
        turned_two[index * half : (index + 1) * half, :] = hidden_two[index].T
    centre_three, scale_three, inverse_wide = get_moments(2, geo.wide_half)

    def finish(rows, carry):
        grad_sum, cross_sum = carry
        normed = (norm_three[rows, :] - centre_three) * scale_three
        norm_three[rows, :] = normed
        before = normed * gain_three + shift_three + x_all[core, rows, :].astype(F32)
        share, slope = gelu_parts(before)
        out_rows[rows, :] = before * share * live_rows(rows, geo.wide_half)
        up = cot_rows[rows, :] * slope
        up_three[rows, :] = up
        return grad_sum + fold_rows(up), cross_sum + fold_rows(up * normed)

    zero_wide = jnp.zeros((8, geo.wide_half), F32)
    send_sums(3, *over_rows(finish, (zero_wide, zero_wide)))
    if geo.scattered:
        to_pair("norm two", 4, norm_two_half, pair_norm_two)
        to_pair("norm one", 2, norm_one_half, pair_norm_one)

    store_count = iter(range(15))

    def store(source, target):
        index = next(store_count)
        copy = pltpu.make_async_copy(source, target, out_sem.at[index])
        copy.start()
        pending["store", index] = copy.wait

    for group in range(3):
        start, real = geo.starts[group], geo.real[group]
        value = out_rows[start : start + real, :].reshape(geo.pixels[group], slots, geo.wide_half)
        raw_out[group][...] = value.astype(BF16)
        store(raw_out[group], outs[group])

    def slopes(up, normed, mask, target, scale, gain, sums, inverse_count, width, plain=None):
        grad_total, cross_total = sums
        factor = gain * scale
        grad_mean, cross_mean = grad_total * inverse_count, cross_total * inverse_count

        def step(rows, carry):
            gap = up[rows, :].astype(F32) - grad_mean - normed[rows, :].astype(F32) * cross_mean
            value = spread(mask[rows, :].astype(F32), width) * (factor * gap)
            if target is not None:
                target[rows, :] = value.astype(BF16)
            if plain is not None:
                plain[pl.ds(pl.multiple_of(GUARD + rows.start, CHUNK), CHUNK), :] = value
            return carry

        over_rows(step, 0)

    def give_affine(index, sums):
        affine_stage[2 * index][...] = sums[1]
        affine_stage[2 * index + 1][...] = sums[0]
        for place in (2 * index, 2 * index + 1):
            store(affine_stage[place], affine_outs[place])

    def owned(which, slot):
        if which == 2:
            return totals[2][slot]
        share = geo.shares[which]
        return totals[which][pl.ds(pl.multiple_of(owner(slot) * share, CHUNK), share), :]

    def reduced(which, slot):
        value = owned(which, slot)
        return value + recv_a[slot].astype(F32) if which == 0 else value

    quarter = wide // 4

    def rs_start(which, stage, piece, source, target, slot):
        copy = pltpu.make_async_remote_copy(
            src_ref=source,
            dst_ref=target,
            send_sem=rs_send.at[which, stage, piece],
            recv_sem=rs_recv.at[which, stage, piece],
            device_id=(owner(slot), core),
            device_id_type=MESH,
        )
        copy.start()
        pending["scatter", which, stage, piece] = copy.wait_recv
        pending["scatter sent", which, stage, piece] = copy.wait_send

    def rs_first():
        for piece in (1, 0):
            low = piece * quarter

            def fill(slot):
                send_a[slot] = owned(0, slot + wide // 2).astype(BF16)

            over_slots(low, low + quarter, fill)
            part = pl.ds(low, quarter)
            rs_start(0, 0, piece, send_a.at[part], recv_a.at[part], wide // 2)

    def rs_second(which):
        send_b, recv_b = staged[which][0:2]
        if which == 0:
            settle(("scatter", 0, 0, 1))
        for slot in reversed(range(quarter)):
            send_b[slot] = reduced(which, slot + quarter).astype(BF16)
            rs_start(which, 1, slot, send_b.at[slot], recv_b.at[slot], quarter)

    def rs_third(which):
        _, recv_b, send_c, recv_c = staged[which]
        if which == 0:
            settle(("scatter", 0, 0, 0))
        for slot in reversed(range(1, quarter)):
            settle(("scatter", which, 1, slot))
            send_c[slot - 1] = (reduced(which, slot) + recv_b[slot].astype(F32)).astype(BF16)
            rs_start(which, 2, slot, send_c.at[slot - 1], recv_c.at[slot - 1], slot)

    def rs_last(which):
        _, recv_b, _, recv_c = staged[which]
        settle(("scatter", which, 1, 0))
        value = reduced(which, 0) + recv_b[0].astype(F32)
        for slot in range(1, quarter):
            settle(("scatter", which, 2, slot))
            value = value + recv_c[slot - 1].astype(F32)
        weight_stage[which][...] = value
        store(weight_stage[which], weight_outs[which])

    sums_three = get_sums(3)
    slopes(
        up_three, norm_three, live, slope_three, scale_three, gain_three, sums_three, inverse_wide, geo.wide_half
    )
    send_two[...] = dot_turned(slope_three[...], conv_last[span(other * half, half), :]).astype(BF16)
    exchange("back two", 5, send_two, recv_two)
    totals[0][...] = dot(turned_two[...], slope_three[...])
    if not geo.scattered:
        store(totals[0], weight_outs[0])
    up_two[...] = dot_turned(slope_three[...], conv_last[span(core * half, half), :])
    give_affine(2, sums_three)
    settle("back two")

    def back_sums(up, halved, received, slope_act, normed):
        def step(rows, carry):
            value = (up[rows, :] + received[rows, :].astype(F32)) * slope_act[rows, :]
            up[rows, :] = value
            if halved is not None:
                halved[rows, :] = value.astype(BF16)
            return carry[0] + fold_rows(value), carry[1] + fold_rows(value * normed[rows, :])

        zero = jnp.zeros((8, half), F32)
        return over_rows(step, (zero, zero))

    half_up_two, half_up_one = (up_two_half, up_one_half) if geo.scattered else (None, None)
    send_sums(4, *back_sums(up_two, half_up_two, recv_two, slope_act_two, norm_two))
    if geo.scattered:
        to_pair("up two", 5, up_two_half, pair_up_two)
        rs_first()
        settle(("pair", "live"), ("pair", "norm two"), ("pair", "turned"))
    sums_two = get_sums(4)
    slopes(up_two, norm_two, live, slope_two, scale_two, gain_two, sums_two, inverse, half, shifted_src)
    if geo.scattered:
        settle(("pair", "up two"))
        slopes(
            pair_up_two, pair_norm_two, pair_live, None, scale_two, gain_two, sums_two, inverse, half, pair_src
        )

    def shift_into(source, position):
        flipped = 8 - position
        for group in range(3):
            start, rows = geo.starts[group], geo.padded[group]
            value = gather_shifted(source, flipped, group)
            if position != 4:
                value = value * spread(shift_masks[flipped, start : start + rows, :], half)
            shifted[start : start + rows, :] = value.astype(BF16)

    def back_parts(low):
        for position in range(9):
            rows = pl.ds(pl.multiple_of(position * geo.hidden + low, half), half)
            parts[position, whole, :] = dot_turned(slope_two[...], conv_middle[rows, :])
        return fold_parts(lambda position: 8 - position)

    for group, value in enumerate(back_parts(other * half)):
        send_one[geo.starts[group] : geo.starts[group] + geo.padded[group], :] = value.astype(BF16)
    exchange("back one", 6, send_one, recv_one)
    for group, value in enumerate(back_parts(core * half)):
        up_one[geo.starts[group] : geo.starts[group] + geo.padded[group], :] = value
    give_affine(1, sums_two)
    settle("back one")

    send_sums(5, *back_sums(up_one, half_up_one, recv_one, slope_act_one, norm_one))
    if geo.scattered:
        to_pair("up one", 6, up_one_half, pair_up_one)
        rs_second(0)
    for position in range(9):
        place = slice(position * geo.hidden, (position + 1) * geo.hidden)
        shift_into(shifted_src, position)
        value = dot(turned_one[...], shifted[...])
        if geo.scattered:
            shift_into(pair_src, position)
            value = value + dot(pair_turned[...], shifted[...])
        totals[1][place, :] = value
    if geo.scattered:
        rs_second(1)
        rs_third(0)
        settle(("pair", "norm one"), ("pair", "x low"), ("pair", "x high"))
    else:
        store(totals[1], weight_outs[1])
    sums_one = get_sums(5)
    slopes(up_one, norm_one, live, slope_one, scale_one, gain_one, sums_one, inverse, half)
    if geo.scattered:
        settle(("pair", "up one"))
        slopes(
            pair_up_one, pair_norm_one, pair_live, pair_slope, scale_one, gain_one, sums_one, inverse, half
        )
        share = geo.shares[2]
        for slot in reversed(range(wide // 2)):
            totals[2][slot] = dot(x_kept[slot], slope_one[...]) + dot(pair_x[slot], pair_slope[...])
        rs_second(2)
    else:
        totals[2][...] = dot(x_kept[...], slope_one[...])
        store(totals[2], weight_outs[2])
    send_in[...] = dot_turned(
        slope_one[...], conv_first[span(other * geo.wide_half, geo.wide_half), :]
    ).astype(BF16)
    exchange("back in", 7, send_in, recv_in)
    if geo.scattered:
        rs_third(1)
    up_three[...] += dot_turned(slope_one[...], conv_first[span(core * geo.wide_half, geo.wide_half), :])
    give_affine(0, sums_one)
    settle("back in")
    for group in range(3):
        start, real, rows = geo.starts[group], geo.real[group], geo.padded[group]
        value = up_three[start : start + rows, :] + recv_in[start : start + rows, :].astype(F32)
        value = value[0:real, :].reshape(geo.pixels[group], slots, geo.wide_half)
        raw_grad[group][...] = value.astype(BF16)
        store(raw_grad[group], in_grads[group])
    if geo.scattered:
        rs_third(2)
        rs_last(0)
        rs_last(1)
        rs_last(2)
    settle_all()


def copy_kernel(count, *refs):
    sources, targets = refs[:count], refs[count : 2 * count]
    held, sem = refs[2 * count : 3 * count], refs[3 * count]
    loads = [pltpu.make_async_copy(sources[i], held[i], sem.at[0, i]) for i in range(count)]
    stores = [pltpu.make_async_copy(held[i], targets[i], sem.at[1, i]) for i in range(count)]
    for load in loads:
        load.start()
    for load, store in zip(loads, stores):
        load.wait()
        store.start()
    for store in stores:
        store.wait()


def run_block(
    wide,
    live_counts,
    small_in,
    mid_in,
    big_in,
    conv_first,
    conv_middle,
    conv_last,
    gain_first,
    shift_first,
    gain_middle,
    shift_middle,
    gain_last,
    shift_last,
    small_cot,
    mid_cot,
    big_cot,
):
    maps = (small_in, mid_in, big_in)
    cots = (small_cot, mid_cot, big_cot)
    channels = 2 * small_in.shape[3]
    hidden, half = conv_last.shape[0], conv_first.shape[1]
    geo = Geometry(wide, [tensor.shape for tensor in maps], channels, hidden, half)
    across = geo.wide_half

    def as_rows(tensor):
        count, height, width, depth = tensor.shape
        return jnp.transpose(tensor, (1, 2, 0, 3)).reshape(height * width, count, depth)

    def as_maps(rows, like):
        count, height, width, depth = like.shape
        return jnp.transpose(rows.reshape(height, width, count, depth), (2, 0, 1, 3))

    affine = [
        vector.reshape(1, -1)
        for vector in (gain_first, shift_first, gain_middle, shift_middle, gain_last, shift_last)
    ]
    operands = [
        live_counts,
        *[as_rows(tensor) for tensor in maps],
        conv_first,
        conv_middle,
        conv_last,
        *affine,
        *[as_rows(tensor) for tensor in cots],
    ]
    raw_shapes = [(count, geo.slots, across) for count in geo.pixels]
    weight_shapes = [(hidden, across), (9 * hidden, half), (channels, half)]
    share_shapes = [
        (share, shape[1]) if geo.scattered else shape
        for share, shape in zip(geo.shares, weight_shapes)
    ]
    out_shapes = [jax.ShapeDtypeStruct(shape, BF16) for shape in raw_shapes * 2]
    out_shapes += [jax.ShapeDtypeStruct(shape, F32) for shape in share_shapes]
    out_shapes += [jax.ShapeDtypeStruct(vector.shape, F32) for vector in affine]

    def vmem(dtype, *shape):
        return pltpu.VMEM(shape, dtype)

    rows, guarded = geo.rows, geo.rows + 2 * GUARD
    scratch = [vmem(BF16, *shape) for shape in raw_shapes * 4]
    scratch += [vmem(BF16, *tensor.shape) for tensor in (conv_first, conv_middle, conv_last)]
    scratch += [vmem(F32, *vector.shape) for vector in affine]
    scratch += [vmem(F32, rows, LANES), vmem(F32, 9, rows, LANES)]
    if geo.scattered:
        x_shapes = [(wide // 2, geo.shares[2], rows)] * 2
    else:
        x_shapes = [(channels, rows), (CHUNK, LANES)]
    scratch += [vmem(BF16, 2, rows, across), *[vmem(BF16, *shape) for shape in x_shapes]]
    scratch += [vmem(F32, rows, across)]
    scratch += [vmem(F32, rows, half), vmem(F32, rows, half), vmem(F32, rows, across)]
    scratch += [vmem(F32, rows, half)] * 2
    scratch += [vmem(BF16, 2, rows, half)] * 2 + [vmem(BF16, hidden, rows)] * 2
    scratch += [vmem(F32, 9, guarded, half), vmem(F32, guarded, half), vmem(BF16, rows, half)]
    scratch += [vmem(F32, rows, across)] * 2 + [vmem(F32, rows, half)] * 2
    scratch += [vmem(BF16, rows, across), vmem(BF16, rows, half), vmem(BF16, rows, half)]
    scratch += [vmem(BF16, rows, half)] * 4 + [vmem(BF16, rows, across)] * 2
    scratch += [
        vmem(F32, wide, 3, half),
        vmem(F32, wide, 2, half),
        vmem(F32, wide, 2, across),
        vmem(F32, wide, 2, across),
        vmem(F32, wide, 2, half),
        vmem(F32, wide, 2, half),
    ]
    total_shapes = list(weight_shapes)
    if geo.scattered:
        total_shapes[2] = (wide // 2, geo.shares[2], half)
    scratch += [vmem(F32, *shape) for shape in total_shapes]
    if geo.scattered:
        scratch += [vmem(BF16, rows, half)] * 5
        scratch += [vmem(BF16, rows, LANES)] + [vmem(BF16, rows, half)] * 4
        scratch += [vmem(BF16, hidden, rows), vmem(BF16, *x_shapes[0]), vmem(F32, guarded, half)]
        scratch += [vmem(BF16, rows, LANES)]
        scratch += [vmem(BF16, wide // 2, geo.shares[0], across)] * 2
        for share, shape in zip(geo.shares, weight_shapes):
            for many in (wide // 4, wide // 4 - 1):
                scratch += [vmem(BF16, many, share, shape[1])] * 2
    scratch += [vmem(F32, *shape) for shape in (share_shapes if geo.scattered else [(8, LANES)] * 3)]
    scratch += [vmem(F32, *vector.shape) for vector in affine]
    dma = pltpu.SemaphoreType.DMA
    scratch += [dma((18,)), dma((15,)), dma((8,)), dma((8,)), dma((6,)), dma((6,))]
    if geo.scattered:
        scratch += [dma((3, 3, wide // 4))] * 2 + [dma((8,))] * 2

    anywhere = pl.BlockSpec(memory_space=pl.ANY)
    results = pl.pallas_call(
        functools.partial(block_kernel, geo),
        out_shape=out_shapes,
        in_specs=[pl.BlockSpec(memory_space=pltpu.SMEM)] + [anywhere] * (len(operands) - 1),
        out_specs=[anywhere] * len(out_shapes),
        scratch_shapes=scratch,
        compiler_params=pltpu.CompilerParams(
            collective_id=0, has_side_effects=True, vmem_limit_bytes=60 * 2**20
        ),
    )(*operands)
    results = pl.pallas_call(
        functools.partial(copy_kernel, len(results)),
        out_shape=[jax.ShapeDtypeStruct(result.shape, result.dtype) for result in results],
        in_specs=[anywhere] * len(results),
        out_specs=[anywhere] * len(results),
        scratch_shapes=[vmem(result.dtype, *result.shape) for result in results]
        + [dma((2, len(results)))],
    )(*results)
    images = [as_maps(rows, like) for rows, like in zip(results[0:6], maps * 2)]
    last_grad, middle_grad, first_grad = results[6:9]
    if not geo.scattered:
        first_grad, middle_grad, last_grad = (
            lax.psum_scatter(grad, "wide", scatter_dimension=0, tiled=True)
            for grad in (first_grad, middle_grad, last_grad)
        )
    vectors = [vector.reshape(-1) for vector in results[9:15]]
    return (*images, first_grad, middle_grad, last_grad, *vectors)


def solution(mesh):
    images = P("wide", None, None, "narrow")
    columns = P(None, "narrow")
    vector = P("narrow")
    return jax.shard_map(
        functools.partial(run_block, mesh.shape["wide"]),
        mesh=mesh,
        in_specs=(P("wide", None),) + (images,) * 3 + (columns,) * 3 + (vector,) * 6 + (images,) * 3,
        out_specs=(images,) * 6 + (P("wide", "narrow"),) * 3 + (vector,) * 6,
        check_vma=False,
    )
```

```python
import functools

import jax
import jax.numpy as jnp
from jax import lax
from jax.experimental import pallas as pl
from jax.experimental.pallas import tpu as pltpu
from jax.sharding import PartitionSpec as P

MESH = pl.DeviceIdType.MESH
EPSILON = 1e-05
F32 = jnp.float32
BF16 = jnp.bfloat16
LANES = 128
CHUNK = 16
GUARD = 64


def ceil_to(value, step):
    return (value + step - 1) // step * step


class Geometry:
    def __init__(self, wide, shapes, channels, hidden, half):
        self.wide = wide
        self.slots = shapes[0][0]
        self.sides = [(shape[1], shape[2]) for shape in shapes]
        self.pixels = [height * width for height, width in self.sides]
        self.real = [count * self.slots for count in self.pixels]
        self.padded = [ceil_to(count, CHUNK) for count in self.real]
        self.starts = [sum(self.padded[:index]) for index in range(len(shapes))]
        self.rows = sum(self.padded)
        self.chunks = self.rows // CHUNK
        self.channels = channels
        self.hidden = hidden
        self.half = half
        self.wide_half = channels // 2
        self.shares = (hidden // wide, 9 * hidden // wide, channels // wide)
        bits = wide.bit_length() - 1
        self.bits = bits
        self.scattered = (
            wide >= 8
            and wide == 1 << bits
            and all(share % CHUNK == 0 for share in self.shares)
            and self.shares[2] % LANES == 0
            and self.wide_half % self.shares[2] == 0
        )


def span(start, size):
    return pl.ds(pl.multiple_of(start, size), size)


def dot(left, right):
    return lax.dot_general(left, right, (((1,), (0,)), ((), ())), preferred_element_type=F32)


def gelu_parts(value):
    share = 0.5 + 0.5 * lax.erf(value * 0.7071067811865476)
    slope = share + value * (jnp.exp(value * value * -0.5) * 0.3989422804014327)
    return share, slope


def block_kernel(geo, *refs):
    refs = list(refs)

    def take(count):
        taken = refs[:count]
        del refs[:count]
        return taken

    (live_counts,) = take(1)
    inputs = take(3)
    first_hbm, middle_hbm, last_hbm = take(3)
    affine_hbm = take(6)
    cots = take(3)
    outs = take(3)
    in_grads = take(3)
    weight_outs = take(3)
    affine_outs = take(6)
    raw_x, raw_cot, raw_out, raw_grad = take(3), take(3), take(3), take(3)
    conv_first, conv_middle, conv_last = take(3)
    first_turned, middle_turned, last_turned = take(3)
    affine = take(6)
    live, shift_masks = take(2)
    x_all, x_kept, x_given, cot_rows = take(4)
    norm_one, norm_two, norm_three = take(3)
    slope_act_one, slope_act_two = take(2)
    hidden_one, hidden_two, turned_one, turned_two = take(4)
    parts, shifted_src, shifted = take(3)
    up_three, out_rows, up_two, up_one = take(4)
    slope_three, slope_two, slope_one = take(3)
    send_two, recv_two, send_one, recv_one, send_in, recv_in = take(6)
    stat_bufs = take(6)
    totals = take(3)
    if geo.scattered:
        norm_one_half, norm_two_half, up_two_half, up_one_half, pair_slope = take(5)
        pair_live, pair_norm_one, pair_norm_two, pair_up_two, pair_up_one = take(5)
        pair_turned, pair_x, pair_src, live_half = take(4)
        send_a, recv_a = take(2)
        staged = [take(4) for _ in range(3)]
    weight_stage = take(3)
    affine_stage = take(6)
    load_sem, out_sem, sib_send, sib_recv, stat_send, stat_recv = take(6)
    if geo.scattered:
        rs_send, rs_recv, pair_send, pair_recv = take(4)
    assert not refs

    wide, slots, half = geo.wide, geo.slots, geo.half
    me = lax.axis_index("wide")
    core = lax.axis_index("narrow")
    other = 1 - core

    pending = {}

    def settle(*keys):
        for key in keys:
            pending.pop(key)()

    def settle_all():
        settle(*list(pending))

    load_count = iter(range(18))

    def load(name, source, target):
        copy = pltpu.make_async_copy(source, target, load_sem.at[next(load_count)])
        copy.start()
        pending[name] = copy.wait

    for group in range(3):
        load(("x", group), inputs[group], raw_x[group])
    load("first", first_hbm, conv_first)
    for index in range(6):
        load(("affine", index), affine_hbm[index], affine[index])
    load("middle", middle_hbm, conv_middle)
    load("last", last_hbm, conv_last)
    for group in range(3):
        load(("cot", group), cots[group], raw_cot[group])

    barrier = pltpu.get_barrier_semaphore()

    def greet(index, carry):
        peer = lax.rem(me + 1 + index, wide)
        pl.semaphore_signal(barrier, inc=1, device_id=(peer, core), device_id_type=MESH)
        return carry

    lax.fori_loop(0, wide - 1, greet, 0)
    pl.semaphore_signal(barrier, inc=1, device_id=(me, other), device_id_type=MESH)

    local_count = 0
    for group in range(3):
        rows = geo.padded[group]
        limit = live_counts[0, group]
        local_count = local_count + limit * geo.pixels[group]
        index = lax.broadcasted_iota(jnp.int32, (rows, LANES), 0)
        image = index % slots
        mask = jnp.where((index < geo.real[group]) & (image < limit), 1.0, 0.0)
        live[geo.starts[group] : geo.starts[group] + rows, :] = mask
        if geo.scattered:
            live_half[geo.starts[group] : geo.starts[group] + rows, :] = mask.astype(BF16)
    count_here = jnp.full((1, LANES), local_count, jnp.int32).astype(F32)

    shift_masks[...] = jnp.ones_like(shift_masks)
    for group in range(3):
        height, width = geo.sides[group]
        start = geo.starts[group]
        line = width * slots
        for position in range(9):
            down, right = position // 3 - 1, position % 3 - 1
            if down == -1:
                shift_masks[position, start : start + line, :] = jnp.zeros((line, LANES), F32)
            if down == 1:
                low = start + (height - 1) * line
                shift_masks[position, low : low + line, :] = jnp.zeros((line, LANES), F32)
            if right:
                for row in range(height):
                    low = start + row * line + (0 if right == -1 else line - slots)
                    shift_masks[position, low : low + slots, :] = jnp.zeros((slots, LANES), F32)
    for buffer in (parts,):
        for position in range(9):
            buffer[position, 0:GUARD, :] = jnp.zeros((GUARD, half), F32)
            buffer[position, GUARD + geo.rows :, :] = jnp.zeros((GUARD, half), F32)
    for buffer in (shifted_src, pair_src) if geo.scattered else (shifted_src,):
        buffer[0:GUARD, :] = jnp.zeros((GUARD, half), F32)
        buffer[GUARD + geo.rows :, :] = jnp.zeros((GUARD, half), F32)

    def spread(tile, width):
        return jnp.concatenate([tile] * (width // LANES), axis=1)

    def live_rows(rows, width):
        return spread(live[rows, :], width)

    def over_rows(body, init, unroll=1):
        return lax.fori_loop(
            0, geo.chunks, lambda step, carry: body(span(step * CHUNK, CHUNK), carry), init, unroll=unroll
        )

    def fold_rows(value):
        return sum(value[index * 8 : index * 8 + 8] for index in range(CHUNK // 8))

    def column_sum(value):
        return jnp.sum(value, axis=0, keepdims=True)

    def weigh(stage):
        if stage == 0:
            return 1 + core
        if stage == 1:
            return 2 - core
        return 1 << stage

    def owner(slot):
        place = me
        for stage in range(geo.bits):
            chosen = (slot // (1 << (geo.bits - 1 - stage))) % 2
            weight = weigh(stage)
            mine = (me // weight) % 2
            place = place + chosen * (1 - 2 * mine) * weight
        return place

    def over_slots(low, high, body):
        lax.fori_loop(low, high, lambda slot, carry: (body(slot), carry)[1], 0)

    def to_pair(name, index, source, target):
        if not geo.scattered:
            return
        copy = pltpu.make_async_remote_copy(
            src_ref=source,
            dst_ref=target,
            send_sem=pair_send.at[index],
            recv_sem=pair_recv.at[index],
            device_id=(owner(wide // 2), core),
            device_id_type=MESH,
        )
        copy.start()
        pending["pair", name] = copy.wait_recv
        pending["pair sent", name] = copy.wait_send

    to_other = {"device_id": (me, other), "device_id_type": MESH}

    def exchange(name, index, source, target):
        copy = pltpu.make_async_remote_copy(
            src_ref=source, dst_ref=target, send_sem=sib_send.at[index], recv_sem=sib_recv.at[index], **to_other
        )
        copy.start()
        pending[name] = copy.wait_recv
        pending[name, "sent"] = copy.wait_send

    for group in range(3):
        settle(("x", group))
        rows, real, start = geo.padded[group], geo.real[group], geo.starts[group]
        value = raw_x[group][...].astype(F32).reshape(real, geo.wide_half)
        if rows > real:
            value = jnp.concatenate([value, jnp.zeros((rows - real, geo.wide_half), F32)], axis=0)
        mask = spread(live[start : start + rows, :], geo.wide_half)
        place = x_all.at[core, pl.ds(start, rows)]
        place[...] = (value * mask).astype(BF16)
    settle("first")
    norm_one[...] = dot(x_all[core], conv_first[span(core * geo.wide_half, geo.wide_half), :])
    pl.semaphore_wait(barrier, wide)
    for group in range(3):
        place = x_all.at[core, pl.ds(geo.starts[group], geo.padded[group])]
        exchange(("x other", group), group, place, place)
    settle(*(("x other", group) for group in range(3)))
    norm_one[...] += dot(x_all[other], conv_first[span(other * geo.wide_half, geo.wide_half), :])

    def broadcast(round_index):
        buffer = stat_bufs[round_index]

        def push(index, carry):
            peer = lax.rem(me + 1 + index, wide)
            pltpu.make_async_remote_copy(
                src_ref=buffer.at[me],
                dst_ref=buffer.at[me],
                send_sem=stat_send.at[round_index],
                recv_sem=stat_recv.at[round_index],
                device_id=(peer, core),
                device_id_type=MESH,
            ).start()
            return carry

        lax.fori_loop(0, wide - 1, push, 0)
        view = buffer.at[pl.ds(0, wide - 1)]
        pending["stat", round_index] = pltpu.make_async_copy(view, view, stat_recv.at[round_index]).wait
        pending["stat sent", round_index] = pltpu.make_async_copy(view, view, stat_send.at[round_index]).wait

    def send_moments(round_index, values, width):
        def add(rows, carry):
            return carry + fold_rows(values[rows, :] * live_rows(rows, width))

        total = column_sum(over_rows(add, jnp.zeros((8, width), F32)))
        centre = total / spread(count_here, width)

        def add_square(rows, carry):
            gap = (values[rows, :] - centre) * live_rows(rows, width)
            return carry + fold_rows(gap * gap)

        squares = column_sum(over_rows(add_square, jnp.zeros((8, width), F32)))
        buffer = stat_bufs[round_index]
        buffer[me, 0:1, :] = total
        buffer[me, 1:2, :] = squares
        if round_index == 0:
            buffer[me, 2:3, :] = spread(count_here, width)
        broadcast(round_index)

    def counts(width):
        return [spread(stat_bufs[0][index, 2:3, 0:LANES], width) for index in range(wide)]

    def get_moments(round_index, width):
        settle(("stat", round_index))
        buffer = stat_bufs[round_index]
        each = counts(width)
        total_count = sum(each)
        centre = sum(buffer[index, 0:1, :] for index in range(wide)) / total_count
        squares = jnp.zeros((1, width), F32)
        for index in range(wide):
            gap = buffer[index, 0:1, :] / each[index] - centre
            squares = squares + (buffer[index, 1:2, :] + each[index] * gap * gap)
        return centre, lax.rsqrt(squares / total_count + EPSILON), 1.0 / total_count

    def send_sums(round_index, first, second):
        buffer = stat_bufs[round_index]
        buffer[me, 0:1, :] = column_sum(first)
        buffer[me, 1:2, :] = column_sum(second)
        broadcast(round_index)

    def get_sums(round_index):
        settle(("stat", round_index))
        buffer = stat_bufs[round_index]
        total = sum(buffer[index] for index in range(wide))
        return total[0:1, :], total[1:2, :]

    def activate(values, halved, slope_act, hidden, centre, scale, gain, shift):
        def step(rows, carry):
            mask = live_rows(rows, half)
            normed = (values[rows, :] - centre) * scale
            values[rows, :] = normed
            if halved is not None:
                halved[rows, :] = normed.astype(BF16)
            act = normed * gain + shift
            share, slope = gelu_parts(act)
            hidden[core, rows, :] = (act * share * mask).astype(BF16)
            slope_act[rows, :] = slope * mask
            return carry

        over_rows(step, 0)

    def gather_shifted(source, position, group):
        width = geo.sides[group][1]
        shift = slots * ((position // 3 - 1) * width + position % 3 - 1)
        low = GUARD + geo.starts[group] + shift
        return source[low : low + geo.padded[group], :]

    def fold_parts(pick):
        results = []
        for group in range(3):
            start, rows = geo.starts[group], geo.padded[group]
            total = None
            for position in range(9):
                value = gather_shifted(parts.at[pick(position)], position, group)
                if position != 4:
                    value = value * spread(shift_masks[position, start : start + rows, :], half)
                total = value if total is None else total + value
            results.append(total)
        return results

    send_moments(0, norm_one, half)
    if geo.scattered:
        share = geo.shares[2]
        per_half = geo.wide_half // share

        def turn(place, slot, target):
            low = pl.multiple_of((place % per_half) * share, share)
            target[slot] = x_all[place // per_half, :, pl.ds(low, share)].T

        many, part = wide // 2, wide // 4
        over_slots(many, many + part, lambda slot: turn(owner(slot), slot - many, x_given))
        low, high = pl.ds(0, part), pl.ds(part, part)
        to_pair("x low", 1, x_given.at[low], pair_x.at[low])
        to_pair("live", 0, live_half, pair_live)
        over_slots(many + part, wide, lambda slot: turn(owner(slot), slot - many, x_given))
        over_slots(0, many, lambda slot: turn(owner(slot), slot, x_kept))
    else:
        for index in range(2):
            x_kept[index * geo.wide_half : (index + 1) * geo.wide_half, :] = x_all[index].T
    for index in range(6):
        settle(("affine", index))
    gain_one, shift_one, gain_two, shift_two, gain_three, shift_three = (ref[...] for ref in affine)
    centre_one, scale_one, inverse = get_moments(0, half)
    half_one, half_two = (norm_one_half, norm_two_half) if geo.scattered else (None, None)
    activate(norm_one, half_one, slope_act_one, hidden_one, centre_one, scale_one, gain_one, shift_one)
    exchange("hidden one", 3, hidden_one.at[core], hidden_one.at[core])
    settle("middle")

    whole = slice(GUARD, GUARD + geo.rows)
    for position in range(9):
        parts[position, whole, :] = dot(
            hidden_one[core], conv_middle[span(position * geo.hidden + core * half, half), :]
        )
    settle("hidden one")
    for position in range(9):
        parts[position, whole, :] += dot(
            hidden_one[other], conv_middle[span(position * geo.hidden + other * half, half), :]
        )
    for group, value in enumerate(fold_parts(lambda position: position)):
        norm_two[geo.starts[group] : geo.starts[group] + geo.padded[group], :] = value
    send_moments(1, norm_two, half)
    if geo.scattered:
        to_pair("x high", 7, x_given.at[high], pair_x.at[high])
    for index in range(2):
        turned_one[index * half : (index + 1) * half, :] = hidden_one[index].T
    for group in range(3):
        settle(("cot", group))
        rows, real, start = geo.padded[group], geo.real[group], geo.starts[group]
        value = raw_cot[group][...].astype(F32).reshape(real, geo.wide_half)
        if rows > real:
            value = jnp.concatenate([value, jnp.zeros((rows - real, geo.wide_half), F32)], axis=0)
        cot_rows[start : start + rows, :] = value * spread(live[start : start + rows, :], geo.wide_half)
    for index in range(18):
        middle_turned[index] = conv_middle[index * half : (index + 1) * half, :].T
    centre_two, scale_two, _ = get_moments(1, half)
    activate(norm_two, half_two, slope_act_two, hidden_two, centre_two, scale_two, gain_two, shift_two)
    exchange("hidden two", 4, hidden_two.at[core], hidden_two.at[core])
    settle("last")
    norm_three[...] = dot(hidden_two[core], conv_last[span(core * half, half), :])
    settle("hidden two")
    norm_three[...] += dot(hidden_two[other], conv_last[span(other * half, half), :])
    send_moments(2, norm_three, geo.wide_half)
    if geo.scattered:
        to_pair("turned", 3, turned_one, pair_turned)
    for index in range(2):
        turned_two[index * half : (index + 1) * half, :] = hidden_two[index].T
    for index in range(2):
        last_turned[index] = conv_last[index * half : (index + 1) * half, :].T
        first_turned[index] = conv_first[index * geo.wide_half : (index + 1) * geo.wide_half, :].T
    centre_three, scale_three, inverse_wide = get_moments(2, geo.wide_half)

    def finish(rows, carry):
        grad_sum, cross_sum = carry
        normed = (norm_three[rows, :] - centre_three) * scale_three
        norm_three[rows, :] = normed
        before = normed * gain_three + shift_three + x_all[core, rows, :].astype(F32)
        share, slope = gelu_parts(before)
        out_rows[rows, :] = before * share * live_rows(rows, geo.wide_half)
        up = cot_rows[rows, :] * slope
        up_three[rows, :] = up
        return grad_sum + fold_rows(up), cross_sum + fold_rows(up * normed)

    zero_wide = jnp.zeros((8, geo.wide_half), F32)
    send_sums(3, *over_rows(finish, (zero_wide, zero_wide)))
    if geo.scattered:
        to_pair("norm two", 4, norm_two_half, pair_norm_two)
        to_pair("norm one", 2, norm_one_half, pair_norm_one)

    store_count = iter(range(15))

    def store(source, target):
        index = next(store_count)
        copy = pltpu.make_async_copy(source, target, out_sem.at[index])
        copy.start()
        pending["store", index] = copy.wait

    for group in range(3):
        start, real = geo.starts[group], geo.real[group]
        value = out_rows[start : start + real, :].reshape(geo.pixels[group], slots, geo.wide_half)
        raw_out[group][...] = value.astype(BF16)
        store(raw_out[group], outs[group])

    def slopes(up, normed, mask, target, scale, gain, sums, inverse_count, width, plain=None):
        grad_total, cross_total = sums
        factor = gain * scale
        grad_mean, cross_mean = grad_total * inverse_count, cross_total * inverse_count

        def step(rows, carry):
            gap = up[rows, :].astype(F32) - grad_mean - normed[rows, :].astype(F32) * cross_mean
            value = spread(mask[rows, :].astype(F32), width) * (factor * gap)
            if target is not None:
                target[rows, :] = value.astype(BF16)
            if plain is not None:
                plain[pl.ds(pl.multiple_of(GUARD + rows.start, CHUNK), CHUNK), :] = value
            return carry

        over_rows(step, 0)

    def give_affine(index, sums):
        affine_stage[2 * index][...] = sums[1]
        affine_stage[2 * index + 1][...] = sums[0]
        for place in (2 * index, 2 * index + 1):
            store(affine_stage[place], affine_outs[place])

    def owned(which, slot):
        if which == 2:
            return totals[2][slot]
        share = geo.shares[which]
        return totals[which][pl.ds(pl.multiple_of(owner(slot) * share, CHUNK), share), :]

    def reduced(which, slot):
        value = owned(which, slot)
        return value + recv_a[slot].astype(F32) if which == 0 else value

    quarter = wide // 4

    def rs_start(which, stage, piece, source, target, slot):
        copy = pltpu.make_async_remote_copy(
            src_ref=source,
            dst_ref=target,
            send_sem=rs_send.at[which, stage, piece],
            recv_sem=rs_recv.at[which, stage, piece],
            device_id=(owner(slot), core),
            device_id_type=MESH,
        )
        copy.start()
        pending["scatter", which, stage, piece] = copy.wait_recv
        pending["scatter sent", which, stage, piece] = copy.wait_send

    def rs_first(piece):
        low = piece * quarter

        def fill(slot):
            send_a[slot] = owned(0, slot + wide // 2).astype(BF16)

        over_slots(low, low + quarter, fill)
        part = pl.ds(low, quarter)
        rs_start(0, 0, piece, send_a.at[part], recv_a.at[part], wide // 2)

    high_slots = list(reversed(range(quarter // 2, quarter)))
    low_slots = list(reversed(range(quarter // 2)))
    far_slots = [slot for slot in high_slots + low_slots if slot]

    def rs_second(which, slots):
        send_b, recv_b = staged[which][0:2]
        for slot in slots:
            send_b[slot] = reduced(which, slot + quarter).astype(BF16)
            rs_start(which, 1, slot, send_b.at[slot], recv_b.at[slot], quarter)

    def rs_third(which, slots):
        _, recv_b, send_c, recv_c = staged[which]
        for slot in slots:
            settle(("scatter", which, 1, slot))
            send_c[slot - 1] = (reduced(which, slot) + recv_b[slot].astype(F32)).astype(BF16)
            rs_start(which, 2, slot, send_c.at[slot - 1], recv_c.at[slot - 1], slot)

    def rs_last(which):
        _, recv_b, _, recv_c = staged[which]
        settle(("scatter", which, 1, 0))
        value = reduced(which, 0) + recv_b[0].astype(F32)
        for slot in range(1, quarter):
            settle(("scatter", which, 2, slot))
            value = value + recv_c[slot - 1].astype(F32)
        weight_stage[which][...] = value
        store(weight_stage[which], weight_outs[which])

    sums_three = get_sums(3)
    slopes(
        up_three, norm_three, live, slope_three, scale_three, gain_three, sums_three, inverse_wide, geo.wide_half
    )
    send_two[...] = dot(slope_three[...], last_turned[other]).astype(BF16)
    exchange("back two", 5, send_two, recv_two)
    totals[0][...] = dot(turned_two[...], slope_three[...])
    if geo.scattered:
        rs_first(1)
    else:
        store(totals[0], weight_outs[0])
    up_two[...] = dot(slope_three[...], last_turned[core])
    give_affine(2, sums_three)
    settle("back two")

    def back_sums(up, halved, received, slope_act, normed):
        def step(rows, carry):
            value = (up[rows, :] + received[rows, :].astype(F32)) * slope_act[rows, :]
            up[rows, :] = value
            if halved is not None:
                halved[rows, :] = value.astype(BF16)
            return carry[0] + fold_rows(value), carry[1] + fold_rows(value * normed[rows, :])

        zero = jnp.zeros((8, half), F32)
        return over_rows(step, (zero, zero))

    half_up_two, half_up_one = (up_two_half, up_one_half) if geo.scattered else (None, None)
    send_sums(4, *back_sums(up_two, half_up_two, recv_two, slope_act_two, norm_two))
    if geo.scattered:
        to_pair("up two", 5, up_two_half, pair_up_two)
        rs_first(0)
        settle(("scatter", 0, 0, 1))
        rs_second(0, high_slots + low_slots)
        settle(("pair", "live"), ("pair", "norm two"), ("pair", "turned"))
    sums_two = get_sums(4)
    slopes(up_two, norm_two, live, slope_two, scale_two, gain_two, sums_two, inverse, half, shifted_src)
    if geo.scattered:
        settle(("pair", "up two"))
        slopes(
            pair_up_two, pair_norm_two, pair_live, None, scale_two, gain_two, sums_two, inverse, half, pair_src
        )

    def shift_into(source, position):
        flipped = 8 - position
        for group in range(3):
            start, rows = geo.starts[group], geo.padded[group]
            value = gather_shifted(source, flipped, group)
            if position != 4:
                value = value * spread(shift_masks[flipped, start : start + rows, :], half)
            shifted[start : start + rows, :] = value.astype(BF16)

    def back_parts(which_half):
        for position in range(9):
            parts[position, whole, :] = dot(slope_two[...], middle_turned[2 * position + which_half])
        return fold_parts(lambda position: 8 - position)

    for group, value in enumerate(back_parts(other)):
        send_one[geo.starts[group] : geo.starts[group] + geo.padded[group], :] = value.astype(BF16)
    exchange("back one", 6, send_one, recv_one)
    for position in range(9):
        place = slice(position * geo.hidden, (position + 1) * geo.hidden)
        shift_into(shifted_src, position)
        value = dot(turned_one[...], shifted[...])
        if geo.scattered:
            shift_into(pair_src, position)
            value = value + dot(pair_turned[...], shifted[...])
        totals[1][place, :] = value
    if geo.scattered:
        rs_second(1, high_slots)
        settle(("scatter", 0, 0, 0))
        rs_third(0, far_slots[:-1])
    else:
        store(totals[1], weight_outs[1])
    for group, value in enumerate(back_parts(core)):
        up_one[geo.starts[group] : geo.starts[group] + geo.padded[group], :] = value
    give_affine(1, sums_two)
    settle("back one")

    send_sums(5, *back_sums(up_one, half_up_one, recv_one, slope_act_one, norm_one))
    if geo.scattered:
        to_pair("up one", 6, up_one_half, pair_up_one)
        rs_second(1, low_slots)
        rs_third(0, far_slots[-1:])
        rs_third(1, far_slots[:-1])
        settle(("pair", "norm one"), ("pair", "x low"), ("pair", "x high"))
    sums_one = get_sums(5)
    slopes(up_one, norm_one, live, slope_one, scale_one, gain_one, sums_one, inverse, half)
    if geo.scattered:
        settle(("pair", "up one"))
        slopes(
            pair_up_one, pair_norm_one, pair_live, pair_slope, scale_one, gain_one, sums_one, inverse, half
        )
        share = geo.shares[2]
        for slot in reversed(range(wide // 2)):
            totals[2][slot] = dot(x_kept[slot], slope_one[...]) + dot(pair_x[slot], pair_slope[...])
        rs_second(2, high_slots + low_slots)
        rs_third(1, far_slots[-1:])
    else:
        totals[2][...] = dot(x_kept[...], slope_one[...])
        store(totals[2], weight_outs[2])
    send_in[...] = dot(slope_one[...], first_turned[other]).astype(BF16)
    exchange("back in", 7, send_in, recv_in)
    up_three[...] += dot(slope_one[...], first_turned[core])
    give_affine(0, sums_one)
    settle("back in")
    for group in range(3):
        start, real, rows = geo.starts[group], geo.real[group], geo.padded[group]
        value = up_three[start : start + rows, :] + recv_in[start : start + rows, :].astype(F32)
        value = value[0:real, :].reshape(geo.pixels[group], slots, geo.wide_half)
        raw_grad[group][...] = value.astype(BF16)
        store(raw_grad[group], in_grads[group])
    if geo.scattered:
        rs_third(2, far_slots)
        rs_last(0)
        rs_last(1)
        rs_last(2)
    settle_all()


def copy_kernel(count, *refs):
    sources, targets = refs[:count], refs[count : 2 * count]
    held, sem = refs[2 * count : 3 * count], refs[3 * count]
    loads = [pltpu.make_async_copy(sources[i], held[i], sem.at[0, i]) for i in range(count)]
    stores = [pltpu.make_async_copy(held[i], targets[i], sem.at[1, i]) for i in range(count)]
    for load in loads:
        load.start()
    for load, store in zip(loads, stores):
        load.wait()
        store.start()
    for store in stores:
        store.wait()


def run_block(
    wide,
    live_counts,
    small_in,
    mid_in,
    big_in,
    conv_first,
    conv_middle,
    conv_last,
    gain_first,
    shift_first,
    gain_middle,
    shift_middle,
    gain_last,
    shift_last,
    small_cot,
    mid_cot,
    big_cot,
):
    maps = (small_in, mid_in, big_in)
    cots = (small_cot, mid_cot, big_cot)
    channels = 2 * small_in.shape[3]
    hidden, half = conv_last.shape[0], conv_first.shape[1]
    geo = Geometry(wide, [tensor.shape for tensor in maps], channels, hidden, half)
    across = geo.wide_half

    def as_rows(tensor):
        count, height, width, depth = tensor.shape
        return jnp.transpose(tensor, (1, 2, 0, 3)).reshape(height * width, count, depth)

    def as_maps(rows, like):
        count, height, width, depth = like.shape
        return jnp.transpose(rows.reshape(height, width, count, depth), (2, 0, 1, 3))

    affine = [
        vector.reshape(1, -1)
        for vector in (gain_first, shift_first, gain_middle, shift_middle, gain_last, shift_last)
    ]
    operands = [
        live_counts,
        *[as_rows(tensor) for tensor in maps],
        conv_first,
        conv_middle,
        conv_last,
        *affine,
        *[as_rows(tensor) for tensor in cots],
    ]
    raw_shapes = [(count, geo.slots, across) for count in geo.pixels]
    weight_shapes = [(hidden, across), (9 * hidden, half), (channels, half)]
    share_shapes = [
        (share, shape[1]) if geo.scattered else shape
        for share, shape in zip(geo.shares, weight_shapes)
    ]
    out_shapes = [jax.ShapeDtypeStruct(shape, BF16) for shape in raw_shapes * 2]
    out_shapes += [jax.ShapeDtypeStruct(shape, F32) for shape in share_shapes]
    out_shapes += [jax.ShapeDtypeStruct(vector.shape, F32) for vector in affine]

    def vmem(dtype, *shape):
        return pltpu.VMEM(shape, dtype)

    rows, guarded = geo.rows, geo.rows + 2 * GUARD
    scratch = [vmem(BF16, *shape) for shape in raw_shapes * 4]
    scratch += [vmem(BF16, *tensor.shape) for tensor in (conv_first, conv_middle, conv_last)]
    scratch += [vmem(BF16, 2, half, across), vmem(BF16, 18, half, half), vmem(BF16, 2, across, half)]
    scratch += [vmem(F32, *vector.shape) for vector in affine]
    scratch += [vmem(F32, rows, LANES), vmem(F32, 9, rows, LANES)]
    if geo.scattered:
        x_shapes = [(wide // 2, geo.shares[2], rows)] * 2
    else:
        x_shapes = [(channels, rows), (CHUNK, LANES)]
    scratch += [vmem(BF16, 2, rows, across), *[vmem(BF16, *shape) for shape in x_shapes]]
    scratch += [vmem(F32, rows, across)]
    scratch += [vmem(F32, rows, half), vmem(F32, rows, half), vmem(F32, rows, across)]
    scratch += [vmem(F32, rows, half)] * 2
    scratch += [vmem(BF16, 2, rows, half)] * 2 + [vmem(BF16, hidden, rows)] * 2
    scratch += [vmem(F32, 9, guarded, half), vmem(F32, guarded, half), vmem(BF16, rows, half)]
    scratch += [vmem(F32, rows, across)] * 2 + [vmem(F32, rows, half)] * 2
    scratch += [vmem(BF16, rows, across), vmem(BF16, rows, half), vmem(BF16, rows, half)]
    scratch += [vmem(BF16, rows, half)] * 4 + [vmem(BF16, rows, across)] * 2
    scratch += [
        vmem(F32, wide, 3, half),
        vmem(F32, wide, 2, half),
        vmem(F32, wide, 2, across),
        vmem(F32, wide, 2, across),
        vmem(F32, wide, 2, half),
        vmem(F32, wide, 2, half),
    ]
    total_shapes = list(weight_shapes)
    if geo.scattered:
        total_shapes[2] = (wide // 2, geo.shares[2], half)
    scratch += [vmem(F32, *shape) for shape in total_shapes]
    if geo.scattered:
        scratch += [vmem(BF16, rows, half)] * 5
        scratch += [vmem(BF16, rows, LANES)] + [vmem(BF16, rows, half)] * 4
        scratch += [vmem(BF16, hidden, rows), vmem(BF16, *x_shapes[0]), vmem(F32, guarded, half)]
        scratch += [vmem(BF16, rows, LANES)]
        scratch += [vmem(BF16, wide // 2, geo.shares[0], across)] * 2
        for share, shape in zip(geo.shares, weight_shapes):
            for many in (wide // 4, wide // 4 - 1):
                scratch += [vmem(BF16, many, share, shape[1])] * 2
    scratch += [vmem(F32, *shape) for shape in (share_shapes if geo.scattered else [(8, LANES)] * 3)]
    scratch += [vmem(F32, *vector.shape) for vector in affine]
    dma = pltpu.SemaphoreType.DMA
    scratch += [dma((18,)), dma((15,)), dma((8,)), dma((8,)), dma((6,)), dma((6,))]
    if geo.scattered:
        scratch += [dma((3, 3, wide // 4))] * 2 + [dma((8,))] * 2

    anywhere = pl.BlockSpec(memory_space=pl.ANY)
    results = pl.pallas_call(
        functools.partial(block_kernel, geo),
        out_shape=out_shapes,
        in_specs=[pl.BlockSpec(memory_space=pltpu.SMEM)] + [anywhere] * (len(operands) - 1),
        out_specs=[anywhere] * len(out_shapes),
        scratch_shapes=scratch,
        compiler_params=pltpu.CompilerParams(
            collective_id=0, has_side_effects=True, vmem_limit_bytes=60 * 2**20
        ),
    )(*operands)
    results = pl.pallas_call(
        functools.partial(copy_kernel, len(results)),
        out_shape=[jax.ShapeDtypeStruct(result.shape, result.dtype) for result in results],
        in_specs=[anywhere] * len(results),
        out_specs=[anywhere] * len(results),
        scratch_shapes=[vmem(result.dtype, *result.shape) for result in results]
        + [dma((2, len(results)))],
    )(*results)
    images = [as_maps(rows, like) for rows, like in zip(results[0:6], maps * 2)]
    last_grad, middle_grad, first_grad = results[6:9]
    if not geo.scattered:
        first_grad, middle_grad, last_grad = (
            lax.psum_scatter(grad, "wide", scatter_dimension=0, tiled=True)
            for grad in (first_grad, middle_grad, last_grad)
        )
    vectors = [vector.reshape(-1) for vector in results[9:15]]
    return (*images, first_grad, middle_grad, last_grad, *vectors)


def solution(mesh):
    images = P("wide", None, None, "narrow")
    columns = P(None, "narrow")
    vector = P("narrow")
    return jax.shard_map(
        functools.partial(run_block, mesh.shape["wide"]),
        mesh=mesh,
        in_specs=(P("wide", None),) + (images,) * 3 + (columns,) * 3 + (vector,) * 6 + (images,) * 3,
        out_specs=(images,) * 6 + (P("wide", "narrow"),) * 3 + (vector,) * 6,
        check_vma=False,
    )
```

```python
import functools

import jax
import jax.numpy as jnp
from jax import lax
from jax.experimental import pallas as pl
from jax.experimental.pallas import tpu as pltpu
from jax.sharding import PartitionSpec as P

MESH = pl.DeviceIdType.MESH
EPSILON = 1e-05
F32 = jnp.float32
BF16 = jnp.bfloat16
LANES = 128
CHUNK = 16
GUARD = 64


def ceil_to(value, step):
    return (value + step - 1) // step * step


class Geometry:
    def __init__(self, wide, shapes, channels, hidden, half):
        self.wide = wide
        self.slots = shapes[0][0]
        self.sides = [(shape[1], shape[2]) for shape in shapes]
        self.pixels = [height * width for height, width in self.sides]
        self.real = [count * self.slots for count in self.pixels]
        self.padded = [ceil_to(count, CHUNK) for count in self.real]
        self.starts = [sum(self.padded[:index]) for index in range(len(shapes))]
        self.rows = sum(self.padded)
        self.chunks = self.rows // CHUNK
        self.channels = channels
        self.hidden = hidden
        self.half = half
        self.wide_half = channels // 2
        self.shares = (hidden // wide, 9 * hidden // wide, channels // wide)
        bits = wide.bit_length() - 1
        self.bits = bits
        self.scattered = (
            wide >= 8
            and wide == 1 << bits
            and all(share % CHUNK == 0 for share in self.shares)
            and self.shares[2] % LANES == 0
            and self.wide_half % self.shares[2] == 0
        )


def span(start, size):
    return pl.ds(pl.multiple_of(start, size), size)


def dot(left, right):
    return lax.dot_general(left, right, (((1,), (0,)), ((), ())), preferred_element_type=F32)


def gelu_parts(value):
    share = 0.5 + 0.5 * lax.erf(value * 0.7071067811865476)
    slope = share + value * (jnp.exp(value * value * -0.5) * 0.3989422804014327)
    return share, slope


def block_kernel(geo, *refs):
    refs = list(refs)

    def take(count):
        taken = refs[:count]
        del refs[:count]
        return taken

    (live_counts,) = take(1)
    inputs = take(3)
    first_hbm, middle_hbm, last_hbm = take(3)
    affine_hbm = take(6)
    cots = take(3)
    outs = take(3)
    in_grads = take(3)
    weight_outs = take(3)
    affine_outs = take(6)
    raw_x, raw_cot, raw_out, raw_grad = take(3), take(3), take(3), take(3)
    conv_first, conv_middle, conv_last = take(3)
    first_turned, middle_turned, last_turned = take(3)
    affine = take(6)
    live, shift_masks = take(2)
    x_all, x_kept, x_given, cot_rows = take(4)
    norm_one, norm_two, norm_three = take(3)
    slope_act_one, slope_act_two = take(2)
    hidden_one, hidden_two, turned_one, turned_two = take(4)
    parts, shifted_src, shifted = take(3)
    up_three, out_rows, up_two, up_one = take(4)
    slope_three, slope_two, slope_one = take(3)
    send_two, recv_two, send_one, recv_one, send_in, recv_in = take(6)
    stat_bufs = take(6)
    totals = take(3)
    if geo.scattered:
        norm_one_half, norm_two_half, up_two_half, up_one_half, pair_slope = take(5)
        pair_live, pair_norm_one, pair_norm_two, pair_up_two, pair_up_one = take(5)
        pair_turned, pair_x, pair_src, live_half = take(4)
        send_a, recv_a = take(2)
        staged = [take(4) for _ in range(3)]
    weight_stage = take(3)
    affine_stage = take(6)
    load_sem, out_sem, sib_send, sib_recv, stat_send, stat_recv = take(6)
    if geo.scattered:
        rs_send, rs_recv, pair_send, pair_recv = take(4)
    assert not refs

    wide, slots, half = geo.wide, geo.slots, geo.half
    me = lax.axis_index("wide")
    core = lax.axis_index("narrow")
    other = 1 - core

    pending = {}

    def settle(*keys):
        for key in keys:
            pending.pop(key)()

    def settle_all():
        settle(*list(pending))

    load_count = iter(range(18))

    def load(name, source, target):
        copy = pltpu.make_async_copy(source, target, load_sem.at[next(load_count)])
        copy.start()
        pending[name] = copy.wait

    for group in range(3):
        load(("x", group), inputs[group], raw_x[group])
    load("first", first_hbm, conv_first)
    for index in range(6):
        load(("affine", index), affine_hbm[index], affine[index])
    load("middle", middle_hbm, conv_middle)
    load("last", last_hbm, conv_last)
    for group in range(3):
        load(("cot", group), cots[group], raw_cot[group])

    barrier = pltpu.get_barrier_semaphore()

    def greet(index, carry):
        peer = lax.rem(me + 1 + index, wide)
        pl.semaphore_signal(barrier, inc=1, device_id=(peer, core), device_id_type=MESH)
        return carry

    lax.fori_loop(0, wide - 1, greet, 0)
    pl.semaphore_signal(barrier, inc=1, device_id=(me, other), device_id_type=MESH)

    local_count = 0
    for group in range(3):
        rows = geo.padded[group]
        limit = live_counts[0, group]
        local_count = local_count + limit * geo.pixels[group]
        index = lax.broadcasted_iota(jnp.int32, (rows, LANES), 0)
        image = index % slots
        mask = jnp.where((index < geo.real[group]) & (image < limit), 1.0, 0.0)
        live[geo.starts[group] : geo.starts[group] + rows, :] = mask
        if geo.scattered:
            live_half[geo.starts[group] : geo.starts[group] + rows, :] = mask.astype(BF16)
    count_here = jnp.full((1, LANES), local_count, jnp.int32).astype(F32)

    shift_masks[...] = jnp.ones_like(shift_masks)
    for group in range(3):
        height, width = geo.sides[group]
        start = geo.starts[group]
        line = width * slots
        for position in range(9):
            down, right = position // 3 - 1, position % 3 - 1
            if down == -1:
                shift_masks[position, start : start + line, :] = jnp.zeros((line, LANES), F32)
            if down == 1:
                low = start + (height - 1) * line
                shift_masks[position, low : low + line, :] = jnp.zeros((line, LANES), F32)
            if right:
                for row in range(height):
                    low = start + row * line + (0 if right == -1 else line - slots)
                    shift_masks[position, low : low + slots, :] = jnp.zeros((slots, LANES), F32)
    for buffer in (parts,):
        for position in range(9):
            buffer[position, 0:GUARD, :] = jnp.zeros((GUARD, half), F32)
            buffer[position, GUARD + geo.rows :, :] = jnp.zeros((GUARD, half), F32)
    for buffer in (shifted_src, pair_src) if geo.scattered else (shifted_src,):
        buffer[0:GUARD, :] = jnp.zeros((GUARD, half), F32)
        buffer[GUARD + geo.rows :, :] = jnp.zeros((GUARD, half), F32)

    def spread(tile, width):
        return jnp.concatenate([tile] * (width // LANES), axis=1)

    def live_rows(rows, width):
        return spread(live[rows, :], width)

    def over_rows(body, init, unroll=4):
        return lax.fori_loop(
            0, geo.chunks, lambda step, carry: body(span(step * CHUNK, CHUNK), carry), init, unroll=unroll
        )

    def fold_rows(value):
        return sum(value[index * 8 : index * 8 + 8] for index in range(CHUNK // 8))

    def column_sum(value):
        return jnp.sum(value, axis=0, keepdims=True)

    def weigh(stage):
        if stage == 0:
            return 1 + core
        if stage == 1:
            return 2 - core
        return 1 << stage

    def owner(slot):
        place = me
        for stage in range(geo.bits):
            chosen = (slot // (1 << (geo.bits - 1 - stage))) % 2
            weight = weigh(stage)
            mine = (me // weight) % 2
            place = place + chosen * (1 - 2 * mine) * weight
        return place

    def over_slots(low, high, body):
        lax.fori_loop(low, high, lambda slot, carry: (body(slot), carry)[1], 0)

    def to_pair(name, index, source, target):
        if not geo.scattered:
            return
        copy = pltpu.make_async_remote_copy(
            src_ref=source,
            dst_ref=target,
            send_sem=pair_send.at[index],
            recv_sem=pair_recv.at[index],
            device_id=(owner(wide // 2), core),
            device_id_type=MESH,
        )
        copy.start()
        pending["pair", name] = copy.wait_recv
        pending["pair sent", name] = copy.wait_send

    to_other = {"device_id": (me, other), "device_id_type": MESH}

    def exchange(name, index, source, target):
        copy = pltpu.make_async_remote_copy(
            src_ref=source, dst_ref=target, send_sem=sib_send.at[index], recv_sem=sib_recv.at[index], **to_other
        )
        copy.start()
        pending[name] = copy.wait_recv
        pending[name, "sent"] = copy.wait_send

    for group in range(3):
        settle(("x", group))
        rows, real, start = geo.padded[group], geo.real[group], geo.starts[group]
        value = raw_x[group][...].astype(F32).reshape(real, geo.wide_half)
        if rows > real:
            value = jnp.concatenate([value, jnp.zeros((rows - real, geo.wide_half), F32)], axis=0)
        mask = spread(live[start : start + rows, :], geo.wide_half)
        place = x_all.at[core, pl.ds(start, rows)]
        place[...] = (value * mask).astype(BF16)
    settle("first")
    norm_one[...] = dot(x_all[core], conv_first[span(core * geo.wide_half, geo.wide_half), :])
    pl.semaphore_wait(barrier, wide)
    for group in range(3):
        place = x_all.at[core, pl.ds(geo.starts[group], geo.padded[group])]
        exchange(("x other", group), group, place, place)
    settle(*(("x other", group) for group in range(3)))
    norm_one[...] += dot(x_all[other], conv_first[span(other * geo.wide_half, geo.wide_half), :])

    def broadcast(round_index):
        buffer = stat_bufs[round_index]

        def push(index, carry):
            peer = lax.rem(me + 1 + index, wide)
            pltpu.make_async_remote_copy(
                src_ref=buffer.at[me],
                dst_ref=buffer.at[me],
                send_sem=stat_send.at[round_index],
                recv_sem=stat_recv.at[round_index],
                device_id=(peer, core),
                device_id_type=MESH,
            ).start()
            return carry

        lax.fori_loop(0, wide - 1, push, 0)
        view = buffer.at[pl.ds(0, wide - 1)]
        pending["stat", round_index] = pltpu.make_async_copy(view, view, stat_recv.at[round_index]).wait
        pending["stat sent", round_index] = pltpu.make_async_copy(view, view, stat_send.at[round_index]).wait

    def send_moments(round_index, values, width):
        def add(rows, carry):
            return carry + fold_rows(values[rows, :] * live_rows(rows, width))

        total = column_sum(over_rows(add, jnp.zeros((8, width), F32)))
        centre = total / spread(count_here, width)

        def add_square(rows, carry):
            gap = (values[rows, :] - centre) * live_rows(rows, width)
            return carry + fold_rows(gap * gap)

        squares = column_sum(over_rows(add_square, jnp.zeros((8, width), F32)))
        buffer = stat_bufs[round_index]
        buffer[me, 0:1, :] = total
        buffer[me, 1:2, :] = squares
        if round_index == 0:
            buffer[me, 2:3, :] = spread(count_here, width)
        broadcast(round_index)

    def counts(width):
        return [spread(stat_bufs[0][index, 2:3, 0:LANES], width) for index in range(wide)]

    def get_moments(round_index, width):
        settle(("stat", round_index))
        buffer = stat_bufs[round_index]
        each = counts(width)
        total_count = sum(each)
        centre = sum(buffer[index, 0:1, :] for index in range(wide)) / total_count
        squares = jnp.zeros((1, width), F32)
        for index in range(wide):
            gap = buffer[index, 0:1, :] / each[index] - centre
            squares = squares + (buffer[index, 1:2, :] + each[index] * gap * gap)
        return centre, lax.rsqrt(squares / total_count + EPSILON), 1.0 / total_count

    def send_sums(round_index, first, second):
        buffer = stat_bufs[round_index]
        buffer[me, 0:1, :] = column_sum(first)
        buffer[me, 1:2, :] = column_sum(second)
        broadcast(round_index)

    def get_sums(round_index):
        settle(("stat", round_index))
        buffer = stat_bufs[round_index]
        total = sum(buffer[index] for index in range(wide))
        return total[0:1, :], total[1:2, :]

    def activate(values, halved, slope_act, hidden, centre, scale, gain, shift):
        def step(rows, carry):
            mask = live_rows(rows, half)
            normed = (values[rows, :] - centre) * scale
            values[rows, :] = normed
            if halved is not None:
                halved[rows, :] = normed.astype(BF16)
            act = normed * gain + shift
            share, slope = gelu_parts(act)
            hidden[core, rows, :] = (act * share * mask).astype(BF16)
            slope_act[rows, :] = slope * mask
            return carry

        over_rows(step, 0)

    def gather_shifted(source, position, group):
        width = geo.sides[group][1]
        shift = slots * ((position // 3 - 1) * width + position % 3 - 1)
        low = GUARD + geo.starts[group] + shift
        return source[low : low + geo.padded[group], :]

    def fold_parts(pick):
        results = []
        for group in range(3):
            start, rows = geo.starts[group], geo.padded[group]
            total = None
            for position in range(9):
                value = gather_shifted(parts.at[pick(position)], position, group)
                if position != 4:
                    value = value * spread(shift_masks[position, start : start + rows, :], half)
                total = value if total is None else total + value
            results.append(total)
        return results

    send_moments(0, norm_one, half)
    if geo.scattered:
        share = geo.shares[2]
        per_half = geo.wide_half // share

        def turn(place, slot, target):
            low = pl.multiple_of((place % per_half) * share, share)
            target[slot] = x_all[place // per_half, :, pl.ds(low, share)].T

        many, part = wide // 2, wide // 4
        over_slots(many, many + part, lambda slot: turn(owner(slot), slot - many, x_given))
        low, high = pl.ds(0, part), pl.ds(part, part)
        to_pair("x low", 1, x_given.at[low], pair_x.at[low])
        to_pair("live", 0, live_half, pair_live)
        over_slots(many + part, wide, lambda slot: turn(owner(slot), slot - many, x_given))
        over_slots(0, many, lambda slot: turn(owner(slot), slot, x_kept))
    else:
        for index in range(2):
            x_kept[index * geo.wide_half : (index + 1) * geo.wide_half, :] = x_all[index].T
    for index in range(6):
        settle(("affine", index))
    gain_one, shift_one, gain_two, shift_two, gain_three, shift_three = (ref[...] for ref in affine)
    centre_one, scale_one, inverse = get_moments(0, half)
    half_one, half_two = (norm_one_half, norm_two_half) if geo.scattered else (None, None)
    activate(norm_one, half_one, slope_act_one, hidden_one, centre_one, scale_one, gain_one, shift_one)
    exchange("hidden one", 3, hidden_one.at[core], hidden_one.at[core])
    settle("middle")

    whole = slice(GUARD, GUARD + geo.rows)
    for position in range(9):
        parts[position, whole, :] = dot(
            hidden_one[core], conv_middle[span(position * geo.hidden + core * half, half), :]
        )
    settle("hidden one")
    for position in range(9):
        parts[position, whole, :] += dot(
            hidden_one[other], conv_middle[span(position * geo.hidden + other * half, half), :]
        )
    for group, value in enumerate(fold_parts(lambda position: position)):
        norm_two[geo.starts[group] : geo.starts[group] + geo.padded[group], :] = value
    send_moments(1, norm_two, half)
    if geo.scattered:
        to_pair("x high", 7, x_given.at[high], pair_x.at[high])
    for index in range(2):
        turned_one[index * half : (index + 1) * half, :] = hidden_one[index].T
    for group in range(3):
        settle(("cot", group))
        rows, real, start = geo.padded[group], geo.real[group], geo.starts[group]
        value = raw_cot[group][...].astype(F32).reshape(real, geo.wide_half)
        if rows > real:
            value = jnp.concatenate([value, jnp.zeros((rows - real, geo.wide_half), F32)], axis=0)
        cot_rows[start : start + rows, :] = value * spread(live[start : start + rows, :], geo.wide_half)
    for index in range(18):
        middle_turned[index] = conv_middle[index * half : (index + 1) * half, :].T
    centre_two, scale_two, _ = get_moments(1, half)
    activate(norm_two, half_two, slope_act_two, hidden_two, centre_two, scale_two, gain_two, shift_two)
    exchange("hidden two", 4, hidden_two.at[core], hidden_two.at[core])
    settle("last")
    norm_three[...] = dot(hidden_two[core], conv_last[span(core * half, half), :])
    settle("hidden two")
    norm_three[...] += dot(hidden_two[other], conv_last[span(other * half, half), :])
    send_moments(2, norm_three, geo.wide_half)
    if geo.scattered:
        to_pair("turned", 3, turned_one, pair_turned)
    for index in range(2):
        turned_two[index * half : (index + 1) * half, :] = hidden_two[index].T
    for index in range(2):
        last_turned[index] = conv_last[index * half : (index + 1) * half, :].T
        first_turned[index] = conv_first[index * geo.wide_half : (index + 1) * geo.wide_half, :].T
    centre_three, scale_three, inverse_wide = get_moments(2, geo.wide_half)

    def finish(rows, carry):
        grad_sum, cross_sum = carry
        normed = (norm_three[rows, :] - centre_three) * scale_three
        norm_three[rows, :] = normed
        before = normed * gain_three + shift_three + x_all[core, rows, :].astype(F32)
        share, slope = gelu_parts(before)
        out_rows[rows, :] = before * share * live_rows(rows, geo.wide_half)
        up = cot_rows[rows, :] * slope
        up_three[rows, :] = up
        return grad_sum + fold_rows(up), cross_sum + fold_rows(up * normed)

    zero_wide = jnp.zeros((8, geo.wide_half), F32)
    send_sums(3, *over_rows(finish, (zero_wide, zero_wide)))
    if geo.scattered:
        to_pair("norm two", 4, norm_two_half, pair_norm_two)
        to_pair("norm one", 2, norm_one_half, pair_norm_one)

    store_count = iter(range(15))

    def store(source, target):
        index = next(store_count)
        copy = pltpu.make_async_copy(source, target, out_sem.at[index])
        copy.start()
        pending["store", index] = copy.wait

    for group in range(3):
        start, real = geo.starts[group], geo.real[group]
        value = out_rows[start : start + real, :].reshape(geo.pixels[group], slots, geo.wide_half)
        raw_out[group][...] = value.astype(BF16)
        store(raw_out[group], outs[group])

    def slopes(up, normed, mask, target, scale, gain, sums, inverse_count, width, plain=None):
        grad_total, cross_total = sums
        factor = gain * scale
        grad_mean, cross_mean = grad_total * inverse_count, cross_total * inverse_count

        def step(rows, carry):
            gap = up[rows, :].astype(F32) - grad_mean - normed[rows, :].astype(F32) * cross_mean
            value = spread(mask[rows, :].astype(F32), width) * (factor * gap)
            if target is not None:
                target[rows, :] = value.astype(BF16)
            if plain is not None:
                plain[pl.ds(pl.multiple_of(GUARD + rows.start, CHUNK), CHUNK), :] = value
            return carry

        over_rows(step, 0)

    def give_affine(index, sums):
        affine_stage[2 * index][...] = sums[1]
        affine_stage[2 * index + 1][...] = sums[0]
        for place in (2 * index, 2 * index + 1):
            store(affine_stage[place], affine_outs[place])

    def owned(which, slot):
        if which == 2:
            return totals[2][slot]
        share = geo.shares[which]
        return totals[which][pl.ds(pl.multiple_of(owner(slot) * share, CHUNK), share), :]

    def reduced(which, slot):
        value = owned(which, slot)
        return value + recv_a[slot].astype(F32) if which == 0 else value

    quarter = wide // 4

    def rs_start(which, stage, piece, source, target, slot):
        copy = pltpu.make_async_remote_copy(
            src_ref=source,
            dst_ref=target,
            send_sem=rs_send.at[which, stage, piece],
            recv_sem=rs_recv.at[which, stage, piece],
            device_id=(owner(slot), core),
            device_id_type=MESH,
        )
        copy.start()
        pending["scatter", which, stage, piece] = copy.wait_recv
        pending["scatter sent", which, stage, piece] = copy.wait_send

    def rs_first(piece):
        low = piece * quarter

        def fill(slot):
            send_a[slot] = owned(0, slot + wide // 2).astype(BF16)

        over_slots(low, low + quarter, fill)
        part = pl.ds(low, quarter)
        rs_start(0, 0, piece, send_a.at[part], recv_a.at[part], wide // 2)

    high_slots = list(reversed(range(quarter // 2, quarter)))
    low_slots = list(reversed(range(quarter // 2)))
    far_slots = [slot for slot in high_slots + low_slots if slot]

    def rs_second(which, slots):
        send_b, recv_b = staged[which][0:2]
        for slot in slots:
            send_b[slot] = reduced(which, slot + quarter).astype(BF16)
            rs_start(which, 1, slot, send_b.at[slot], recv_b.at[slot], quarter)

    def rs_third(which, slots):
        _, recv_b, send_c, recv_c = staged[which]
        for slot in slots:
            settle(("scatter", which, 1, slot))
            send_c[slot - 1] = (reduced(which, slot) + recv_b[slot].astype(F32)).astype(BF16)
            rs_start(which, 2, slot, send_c.at[slot - 1], recv_c.at[slot - 1], slot)

    def rs_last(which):
        _, recv_b, _, recv_c = staged[which]
        settle(("scatter", which, 1, 0))
        value = reduced(which, 0) + recv_b[0].astype(F32)
        for slot in range(1, quarter):
            settle(("scatter", which, 2, slot))
            value = value + recv_c[slot - 1].astype(F32)
        weight_stage[which][...] = value
        store(weight_stage[which], weight_outs[which])

    sums_three = get_sums(3)
    slopes(
        up_three, norm_three, live, slope_three, scale_three, gain_three, sums_three, inverse_wide, geo.wide_half
    )
    send_two[...] = dot(slope_three[...], last_turned[other]).astype(BF16)
    exchange("back two", 5, send_two, recv_two)
    totals[0][...] = dot(turned_two[...], slope_three[...])
    if geo.scattered:
        rs_first(1)
    else:
        store(totals[0], weight_outs[0])
    up_two[...] = dot(slope_three[...], last_turned[core])
    give_affine(2, sums_three)
    settle("back two")

    def back_sums(up, halved, received, slope_act, normed):
        def step(rows, carry):
            value = (up[rows, :] + received[rows, :].astype(F32)) * slope_act[rows, :]
            up[rows, :] = value
            if halved is not None:
                halved[rows, :] = value.astype(BF16)
            return carry[0] + fold_rows(value), carry[1] + fold_rows(value * normed[rows, :])

        zero = jnp.zeros((8, half), F32)
        return over_rows(step, (zero, zero))

    half_up_two, half_up_one = (up_two_half, up_one_half) if geo.scattered else (None, None)
    send_sums(4, *back_sums(up_two, half_up_two, recv_two, slope_act_two, norm_two))
    if geo.scattered:
        to_pair("up two", 5, up_two_half, pair_up_two)
        rs_first(0)
        settle(("scatter", 0, 0, 1))
        rs_second(0, high_slots + low_slots)
        settle(("pair", "live"), ("pair", "norm two"), ("pair", "turned"))
    sums_two = get_sums(4)
    slopes(up_two, norm_two, live, slope_two, scale_two, gain_two, sums_two, inverse, half, shifted_src)
    if geo.scattered:
        settle(("pair", "up two"))
        slopes(
            pair_up_two, pair_norm_two, pair_live, None, scale_two, gain_two, sums_two, inverse, half, pair_src
        )

    def shift_into(source, position):
        flipped = 8 - position
        for group in range(3):
            start, rows = geo.starts[group], geo.padded[group]
            value = gather_shifted(source, flipped, group)
            if position != 4:
                value = value * spread(shift_masks[flipped, start : start + rows, :], half)
            shifted[start : start + rows, :] = value.astype(BF16)

    def back_parts(which_half):
        for position in range(9):
            parts[position, whole, :] = dot(slope_two[...], middle_turned[2 * position + which_half])
        return fold_parts(lambda position: 8 - position)

    for group, value in enumerate(back_parts(other)):
        send_one[geo.starts[group] : geo.starts[group] + geo.padded[group], :] = value.astype(BF16)
    exchange("back one", 6, send_one, recv_one)
    for position in range(9):
        place = slice(position * geo.hidden, (position + 1) * geo.hidden)
        shift_into(shifted_src, position)
        value = dot(turned_one[...], shifted[...])
        if geo.scattered:
            shift_into(pair_src, position)
            value = value + dot(pair_turned[...], shifted[...])
        totals[1][place, :] = value
    if geo.scattered:
        rs_second(1, high_slots)
        settle(("scatter", 0, 0, 0))
        rs_third(0, far_slots[:-1])
    else:
        store(totals[1], weight_outs[1])
    for group, value in enumerate(back_parts(core)):
        up_one[geo.starts[group] : geo.starts[group] + geo.padded[group], :] = value
    give_affine(1, sums_two)
    settle("back one")

    send_sums(5, *back_sums(up_one, half_up_one, recv_one, slope_act_one, norm_one))
    if geo.scattered:
        to_pair("up one", 6, up_one_half, pair_up_one)
        rs_second(1, low_slots)
        rs_third(0, far_slots[-1:])
        rs_third(1, far_slots[:-1])
        settle(("pair", "norm one"), ("pair", "x low"), ("pair", "x high"))
    sums_one = get_sums(5)
    slopes(up_one, norm_one, live, slope_one, scale_one, gain_one, sums_one, inverse, half)
    if geo.scattered:
        settle(("pair", "up one"))
        slopes(
            pair_up_one, pair_norm_one, pair_live, pair_slope, scale_one, gain_one, sums_one, inverse, half
        )
        share = geo.shares[2]
        for slot in reversed(range(wide // 2)):
            totals[2][slot] = dot(x_kept[slot], slope_one[...]) + dot(pair_x[slot], pair_slope[...])
        rs_second(2, high_slots + low_slots)
        rs_third(1, far_slots[-1:])
    else:
        totals[2][...] = dot(x_kept[...], slope_one[...])
        store(totals[2], weight_outs[2])
    send_in[...] = dot(slope_one[...], first_turned[other]).astype(BF16)
    exchange("back in", 7, send_in, recv_in)
    up_three[...] += dot(slope_one[...], first_turned[core])
    give_affine(0, sums_one)
    settle("back in")
    for group in range(3):
        start, real, rows = geo.starts[group], geo.real[group], geo.padded[group]
        value = up_three[start : start + rows, :] + recv_in[start : start + rows, :].astype(F32)
        value = value[0:real, :].reshape(geo.pixels[group], slots, geo.wide_half)
        raw_grad[group][...] = value.astype(BF16)
        store(raw_grad[group], in_grads[group])
    if geo.scattered:
        rs_third(2, far_slots)
        rs_last(0)
        rs_last(1)
        rs_last(2)
    settle_all()


def copy_kernel(count, *refs):
    sources, targets = refs[:count], refs[count : 2 * count]
    held, sem = refs[2 * count : 3 * count], refs[3 * count]
    loads = [pltpu.make_async_copy(sources[i], held[i], sem.at[0, i]) for i in range(count)]
    stores = [pltpu.make_async_copy(held[i], targets[i], sem.at[1, i]) for i in range(count)]
    for load in loads:
        load.start()
    for load, store in zip(loads, stores):
        load.wait()
        store.start()
    for store in stores:
        store.wait()


def run_block(
    wide,
    live_counts,
    small_in,
    mid_in,
    big_in,
    conv_first,
    conv_middle,
    conv_last,
    gain_first,
    shift_first,
    gain_middle,
    shift_middle,
    gain_last,
    shift_last,
    small_cot,
    mid_cot,
    big_cot,
):
    maps = (small_in, mid_in, big_in)
    cots = (small_cot, mid_cot, big_cot)
    channels = 2 * small_in.shape[3]
    hidden, half = conv_last.shape[0], conv_first.shape[1]
    geo = Geometry(wide, [tensor.shape for tensor in maps], channels, hidden, half)
    across = geo.wide_half

    def as_rows(tensor):
        count, height, width, depth = tensor.shape
        return jnp.transpose(tensor, (1, 2, 0, 3)).reshape(height * width, count, depth)

    def as_maps(rows, like):
        count, height, width, depth = like.shape
        return jnp.transpose(rows.reshape(height, width, count, depth), (2, 0, 1, 3))

    affine = [
        vector.reshape(1, -1)
        for vector in (gain_first, shift_first, gain_middle, shift_middle, gain_last, shift_last)
    ]
    operands = [
        live_counts,
        *[as_rows(tensor) for tensor in maps],
        conv_first,
        conv_middle,
        conv_last,
        *affine,
        *[as_rows(tensor) for tensor in cots],
    ]
    raw_shapes = [(count, geo.slots, across) for count in geo.pixels]
    weight_shapes = [(hidden, across), (9 * hidden, half), (channels, half)]
    share_shapes = [
        (share, shape[1]) if geo.scattered else shape
        for share, shape in zip(geo.shares, weight_shapes)
    ]
    out_shapes = [jax.ShapeDtypeStruct(shape, BF16) for shape in raw_shapes * 2]
    out_shapes += [jax.ShapeDtypeStruct(shape, F32) for shape in share_shapes]
    out_shapes += [jax.ShapeDtypeStruct(vector.shape, F32) for vector in affine]

    def vmem(dtype, *shape):
        return pltpu.VMEM(shape, dtype)

    rows, guarded = geo.rows, geo.rows + 2 * GUARD
    scratch = [vmem(BF16, *shape) for shape in raw_shapes * 4]
    scratch += [vmem(BF16, *tensor.shape) for tensor in (conv_first, conv_middle, conv_last)]
    scratch += [vmem(BF16, 2, half, across), vmem(BF16, 18, half, half), vmem(BF16, 2, across, half)]
    scratch += [vmem(F32, *vector.shape) for vector in affine]
    scratch += [vmem(F32, rows, LANES), vmem(F32, 9, rows, LANES)]
    if geo.scattered:
        x_shapes = [(wide // 2, geo.shares[2], rows)] * 2
    else:
        x_shapes = [(channels, rows), (CHUNK, LANES)]
    scratch += [vmem(BF16, 2, rows, across), *[vmem(BF16, *shape) for shape in x_shapes]]
    scratch += [vmem(F32, rows, across)]
    scratch += [vmem(F32, rows, half), vmem(F32, rows, half), vmem(F32, rows, across)]
    scratch += [vmem(F32, rows, half)] * 2
    scratch += [vmem(BF16, 2, rows, half)] * 2 + [vmem(BF16, hidden, rows)] * 2
    scratch += [vmem(F32, 9, guarded, half), vmem(F32, guarded, half), vmem(BF16, rows, half)]
    scratch += [vmem(F32, rows, across)] * 2 + [vmem(F32, rows, half)] * 2
    scratch += [vmem(BF16, rows, across), vmem(BF16, rows, half), vmem(BF16, rows, half)]
    scratch += [vmem(BF16, rows, half)] * 4 + [vmem(BF16, rows, across)] * 2
    scratch += [
        vmem(F32, wide, 3, half),
        vmem(F32, wide, 2, half),
        vmem(F32, wide, 2, across),
        vmem(F32, wide, 2, across),
        vmem(F32, wide, 2, half),
        vmem(F32, wide, 2, half),
    ]
    total_shapes = list(weight_shapes)
    if geo.scattered:
        total_shapes[2] = (wide // 2, geo.shares[2], half)
    scratch += [vmem(F32, *shape) for shape in total_shapes]
    if geo.scattered:
        scratch += [vmem(BF16, rows, half)] * 5
        scratch += [vmem(BF16, rows, LANES)] + [vmem(BF16, rows, half)] * 4
        scratch += [vmem(BF16, hidden, rows), vmem(BF16, *x_shapes[0]), vmem(F32, guarded, half)]
        scratch += [vmem(BF16, rows, LANES)]
        scratch += [vmem(BF16, wide // 2, geo.shares[0], across)] * 2
        for share, shape in zip(geo.shares, weight_shapes):
            for many in (wide // 4, wide // 4 - 1):
                scratch += [vmem(BF16, many, share, shape[1])] * 2
    scratch += [vmem(F32, *shape) for shape in (share_shapes if geo.scattered else [(8, LANES)] * 3)]
    scratch += [vmem(F32, *vector.shape) for vector in affine]
    dma = pltpu.SemaphoreType.DMA
    scratch += [dma((18,)), dma((15,)), dma((8,)), dma((8,)), dma((6,)), dma((6,))]
    if geo.scattered:
        scratch += [dma((3, 3, wide // 4))] * 2 + [dma((8,))] * 2

    anywhere = pl.BlockSpec(memory_space=pl.ANY)
    results = pl.pallas_call(
        functools.partial(block_kernel, geo),
        out_shape=out_shapes,
        in_specs=[pl.BlockSpec(memory_space=pltpu.SMEM)] + [anywhere] * (len(operands) - 1),
        out_specs=[anywhere] * len(out_shapes),
        scratch_shapes=scratch,
        compiler_params=pltpu.CompilerParams(
            collective_id=0, has_side_effects=True, vmem_limit_bytes=60 * 2**20
        ),
    )(*operands)
    results = pl.pallas_call(
        functools.partial(copy_kernel, len(results)),
        out_shape=[jax.ShapeDtypeStruct(result.shape, result.dtype) for result in results],
        in_specs=[anywhere] * len(results),
        out_specs=[anywhere] * len(results),
        scratch_shapes=[vmem(result.dtype, *result.shape) for result in results]
        + [dma((2, len(results)))],
    )(*results)
    images = [as_maps(rows, like) for rows, like in zip(results[0:6], maps * 2)]
    last_grad, middle_grad, first_grad = results[6:9]
    if not geo.scattered:
        first_grad, middle_grad, last_grad = (
            lax.psum_scatter(grad, "wide", scatter_dimension=0, tiled=True)
            for grad in (first_grad, middle_grad, last_grad)
        )
    vectors = [vector.reshape(-1) for vector in results[9:15]]
    return (*images, first_grad, middle_grad, last_grad, *vectors)


def solution(mesh):
    images = P("wide", None, None, "narrow")
    columns = P(None, "narrow")
    vector = P("narrow")
    return jax.shard_map(
        functools.partial(run_block, mesh.shape["wide"]),
        mesh=mesh,
        in_specs=(P("wide", None),) + (images,) * 3 + (columns,) * 3 + (vector,) * 6 + (images,) * 3,
        out_specs=(images,) * 6 + (P("wide", "narrow"),) * 3 + (vector,) * 6,
        check_vma=False,
    )
```

```python
import functools

import jax
import jax.numpy as jnp
from jax import lax
from jax.experimental import pallas as pl
from jax.experimental.pallas import tpu as pltpu
from jax.sharding import PartitionSpec as P

MESH = pl.DeviceIdType.MESH
EPSILON = 1e-05
F32 = jnp.float32
BF16 = jnp.bfloat16
LANES = 128
CHUNK = 16
GUARD = 64


def ceil_to(value, step):
    return (value + step - 1) // step * step


class Geometry:
    def __init__(self, wide, shapes, channels, hidden, half):
        self.wide = wide
        self.slots = shapes[0][0]
        self.sides = [(shape[1], shape[2]) for shape in shapes]
        self.pixels = [height * width for height, width in self.sides]
        self.real = [count * self.slots for count in self.pixels]
        self.padded = [ceil_to(count, CHUNK) for count in self.real]
        self.starts = [sum(self.padded[:index]) for index in range(len(shapes))]
        self.rows = sum(self.padded)
        self.chunks = self.rows // CHUNK
        self.channels = channels
        self.hidden = hidden
        self.half = half
        self.wide_half = channels // 2
        self.shares = (hidden // wide, 9 * hidden // wide, channels // wide)
        bits = wide.bit_length() - 1
        self.bits = bits
        self.scattered = (
            wide >= 8
            and wide == 1 << bits
            and all(share % CHUNK == 0 for share in self.shares)
            and self.shares[2] % LANES == 0
            and self.wide_half % self.shares[2] == 0
        )


def span(start, size):
    return pl.ds(pl.multiple_of(start, size), size)


def dot(left, right):
    return lax.dot_general(left, right, (((1,), (0,)), ((), ())), preferred_element_type=F32)


def gelu_parts(value):
    share = 0.5 + 0.5 * lax.erf(value * 0.7071067811865476)
    slope = share + value * (jnp.exp(value * value * -0.5) * 0.3989422804014327)
    return share, slope


def block_kernel(geo, *refs):
    refs = list(refs)

    def take(count):
        taken = refs[:count]
        del refs[:count]
        return taken

    (live_counts,) = take(1)
    inputs = take(3)
    first_hbm, middle_hbm, last_hbm = take(3)
    affine_hbm = take(6)
    cots = take(3)
    outs = take(3)
    in_grads = take(3)
    weight_outs = take(3)
    affine_outs = take(6)
    raw_x, raw_cot, raw_out, raw_grad = take(3), take(3), take(3), take(3)
    conv_first, conv_middle, conv_last = take(3)
    first_turned, middle_turned, last_turned = take(3)
    affine = take(6)
    live, shift_masks = take(2)
    x_all, x_kept, x_given, cot_rows = take(4)
    norm_one, norm_two, norm_three = take(3)
    slope_act_one, slope_act_two = take(2)
    hidden_one, hidden_two, turned_one, turned_two = take(4)
    parts, shifted_src, shifted = take(3)
    up_three, out_rows, up_two, up_one = take(4)
    slope_three, slope_two, slope_one = take(3)
    send_two, recv_two, send_one, recv_one, send_in, recv_in = take(6)
    stat_bufs = take(6)
    totals = take(3)
    if geo.scattered:
        norm_one_half, norm_two_half, up_two_half, up_one_half, pair_slope = take(5)
        pair_live, pair_norm_one, pair_norm_two, pair_up_two, pair_up_one = take(5)
        pair_turned, pair_x, pair_src, live_half = take(4)
        send_a, recv_a = take(2)
        staged = [take(4) for _ in range(3)]
    weight_stage = take(3)
    affine_stage = take(6)
    load_sem, out_sem, sib_send, sib_recv, stat_send, stat_recv = take(6)
    if geo.scattered:
        rs_send, rs_recv, pair_send, pair_recv = take(4)
    assert not refs

    wide, slots, half = geo.wide, geo.slots, geo.half
    me = lax.axis_index("wide")
    core = lax.axis_index("narrow")
    other = 1 - core

    pending = {}

    def settle(*keys):
        for key in keys:
            pending.pop(key)()

    def settle_all():
        settle(*list(pending))

    load_count = iter(range(18))

    def load(name, source, target):
        copy = pltpu.make_async_copy(source, target, load_sem.at[next(load_count)])
        copy.start()
        pending[name] = copy.wait

    for group in range(3):
        load(("x", group), inputs[group], raw_x[group])
    load("first", first_hbm, conv_first)
    for index in range(6):
        load(("affine", index), affine_hbm[index], affine[index])
    load("middle", middle_hbm, conv_middle)
    load("last", last_hbm, conv_last)
    for group in range(3):
        load(("cot", group), cots[group], raw_cot[group])

    barrier = pltpu.get_barrier_semaphore()

    def greet(index, carry):
        peer = lax.rem(me + 1 + index, wide)
        pl.semaphore_signal(barrier, inc=1, device_id=(peer, core), device_id_type=MESH)
        return carry

    lax.fori_loop(0, wide - 1, greet, 0)
    pl.semaphore_signal(barrier, inc=1, device_id=(me, other), device_id_type=MESH)

    local_count = 0
    for group in range(3):
        rows = geo.padded[group]
        limit = live_counts[0, group]
        local_count = local_count + limit * geo.pixels[group]
        index = lax.broadcasted_iota(jnp.int32, (rows, LANES), 0)
        image = index % slots
        mask = jnp.where((index < geo.real[group]) & (image < limit), 1.0, 0.0)
        live[geo.starts[group] : geo.starts[group] + rows, :] = mask
        if geo.scattered:
            live_half[geo.starts[group] : geo.starts[group] + rows, :] = mask.astype(BF16)
    count_here = jnp.full((1, LANES), local_count, jnp.int32).astype(F32)

    shift_masks[...] = jnp.ones_like(shift_masks)
    for group in range(3):
        height, width = geo.sides[group]
        start = geo.starts[group]
        line = width * slots
        for position in range(9):
            down, right = position // 3 - 1, position % 3 - 1
            if down == -1:
                shift_masks[position, start : start + line, :] = jnp.zeros((line, LANES), F32)
            if down == 1:
                low = start + (height - 1) * line
                shift_masks[position, low : low + line, :] = jnp.zeros((line, LANES), F32)
            if right:
                for row in range(height):
                    low = start + row * line + (0 if right == -1 else line - slots)
                    shift_masks[position, low : low + slots, :] = jnp.zeros((slots, LANES), F32)
    for buffer in (parts,):
        for position in range(9):
            buffer[position, 0:GUARD, :] = jnp.zeros((GUARD, half), F32)
            buffer[position, GUARD + geo.rows :, :] = jnp.zeros((GUARD, half), F32)
    for buffer in (shifted_src, pair_src) if geo.scattered else (shifted_src,):
        buffer[0:GUARD, :] = jnp.zeros((GUARD, half), F32)
        buffer[GUARD + geo.rows :, :] = jnp.zeros((GUARD, half), F32)

    def spread(tile, width):
        return jnp.concatenate([tile] * (width // LANES), axis=1)

    def live_rows(rows, width):
        return spread(live[rows, :], width)

    def over_rows(body, init, unroll=geo.chunks):
        return lax.fori_loop(
            0, geo.chunks, lambda step, carry: body(span(step * CHUNK, CHUNK), carry), init, unroll=unroll
        )

    def fold_rows(value):
        return sum(value[index * 8 : index * 8 + 8] for index in range(CHUNK // 8))

    def column_sum(value):
        return jnp.sum(value, axis=0, keepdims=True)

    def weigh(stage):
        if stage == 0:
            return 1 + core
        if stage == 1:
            return 2 - core
        return 1 << stage

    def owner(slot):
        place = me
        for stage in range(geo.bits):
            chosen = (slot // (1 << (geo.bits - 1 - stage))) % 2
            weight = weigh(stage)
            mine = (me // weight) % 2
            place = place + chosen * (1 - 2 * mine) * weight
        return place

    def over_slots(low, high, body):
        lax.fori_loop(low, high, lambda slot, carry: (body(slot), carry)[1], 0)

    def to_pair(name, index, source, target):
        if not geo.scattered:
            return
        copy = pltpu.make_async_remote_copy(
            src_ref=source,
            dst_ref=target,
            send_sem=pair_send.at[index],
            recv_sem=pair_recv.at[index],
            device_id=(owner(wide // 2), core),
            device_id_type=MESH,
        )
        copy.start()
        pending["pair", name] = copy.wait_recv
        pending["pair sent", name] = copy.wait_send

    to_other = {"device_id": (me, other), "device_id_type": MESH}

    def exchange(name, index, source, target):
        copy = pltpu.make_async_remote_copy(
            src_ref=source, dst_ref=target, send_sem=sib_send.at[index], recv_sem=sib_recv.at[index], **to_other
        )
        copy.start()
        pending[name] = copy.wait_recv
        pending[name, "sent"] = copy.wait_send

    for group in range(3):
        settle(("x", group))
        rows, real, start = geo.padded[group], geo.real[group], geo.starts[group]
        value = raw_x[group][...].astype(F32).reshape(real, geo.wide_half)
        if rows > real:
            value = jnp.concatenate([value, jnp.zeros((rows - real, geo.wide_half), F32)], axis=0)
        mask = spread(live[start : start + rows, :], geo.wide_half)
        place = x_all.at[core, pl.ds(start, rows)]
        place[...] = (value * mask).astype(BF16)
    settle("first")
    norm_one[...] = dot(x_all[core], conv_first[span(core * geo.wide_half, geo.wide_half), :])
    pl.semaphore_wait(barrier, wide)
    for group in range(3):
        place = x_all.at[core, pl.ds(geo.starts[group], geo.padded[group])]
        exchange(("x other", group), group, place, place)
    settle(*(("x other", group) for group in range(3)))
    norm_one[...] += dot(x_all[other], conv_first[span(other * geo.wide_half, geo.wide_half), :])

    def broadcast(round_index):
        buffer = stat_bufs[round_index]

        def push(index, carry):
            peer = lax.rem(me + 1 + index, wide)
            pltpu.make_async_remote_copy(
                src_ref=buffer.at[me],
                dst_ref=buffer.at[me],
                send_sem=stat_send.at[round_index],
                recv_sem=stat_recv.at[round_index],
                device_id=(peer, core),
                device_id_type=MESH,
            ).start()
            return carry

        lax.fori_loop(0, wide - 1, push, 0)
        view = buffer.at[pl.ds(0, wide - 1)]
        pending["stat", round_index] = pltpu.make_async_copy(view, view, stat_recv.at[round_index]).wait
        pending["stat sent", round_index] = pltpu.make_async_copy(view, view, stat_send.at[round_index]).wait

    def send_moments(round_index, values, width):
        def add(rows, carry):
            return carry + fold_rows(values[rows, :] * live_rows(rows, width))

        total = column_sum(over_rows(add, jnp.zeros((8, width), F32)))
        centre = total / spread(count_here, width)

        def add_square(rows, carry):
            gap = (values[rows, :] - centre) * live_rows(rows, width)
            return carry + fold_rows(gap * gap)

        squares = column_sum(over_rows(add_square, jnp.zeros((8, width), F32)))
        buffer = stat_bufs[round_index]
        buffer[me, 0:1, :] = total
        buffer[me, 1:2, :] = squares
        if round_index == 0:
            buffer[me, 2:3, :] = spread(count_here, width)
        broadcast(round_index)

    def counts(width):
        return [spread(stat_bufs[0][index, 2:3, 0:LANES], width) for index in range(wide)]

    def get_moments(round_index, width):
        settle(("stat", round_index))
        buffer = stat_bufs[round_index]
        each = counts(width)
        total_count = sum(each)
        centre = sum(buffer[index, 0:1, :] for index in range(wide)) / total_count
        squares = jnp.zeros((1, width), F32)
        for index in range(wide):
            gap = buffer[index, 0:1, :] / each[index] - centre
            squares = squares + (buffer[index, 1:2, :] + each[index] * gap * gap)
        return centre, lax.rsqrt(squares / total_count + EPSILON), 1.0 / total_count

    def send_sums(round_index, first, second):
        buffer = stat_bufs[round_index]
        buffer[me, 0:1, :] = column_sum(first)
        buffer[me, 1:2, :] = column_sum(second)
        broadcast(round_index)

    def get_sums(round_index):
        settle(("stat", round_index))
        buffer = stat_bufs[round_index]
        total = sum(buffer[index] for index in range(wide))
        return total[0:1, :], total[1:2, :]

    def activate(values, halved, slope_act, hidden, centre, scale, gain, shift):
        def step(rows, carry):
            mask = live_rows(rows, half)
            normed = (values[rows, :] - centre) * scale
            values[rows, :] = normed
            if halved is not None:
                halved[rows, :] = normed.astype(BF16)
            act = normed * gain + shift
            share, slope = gelu_parts(act)
            hidden[core, rows, :] = (act * share * mask).astype(BF16)
            slope_act[rows, :] = slope * mask
            return carry

        over_rows(step, 0)

    def gather_shifted(source, position, group):
        width = geo.sides[group][1]
        shift = slots * ((position // 3 - 1) * width + position % 3 - 1)
        low = GUARD + geo.starts[group] + shift
        return source[low : low + geo.padded[group], :]

    def fold_parts(pick):
        results = []
        for group in range(3):
            start, rows = geo.starts[group], geo.padded[group]
            total = None
            for position in range(9):
                value = gather_shifted(parts.at[pick(position)], position, group)
                if position != 4:
                    value = value * spread(shift_masks[position, start : start + rows, :], half)
                total = value if total is None else total + value
            results.append(total)
        return results

    send_moments(0, norm_one, half)
    if geo.scattered:
        share = geo.shares[2]
        per_half = geo.wide_half // share

        def turn(place, slot, target):
            low = pl.multiple_of((place % per_half) * share, share)
            target[slot] = x_all[place // per_half, :, pl.ds(low, share)].T

        many, part = wide // 2, wide // 4
        over_slots(many, many + part, lambda slot: turn(owner(slot), slot - many, x_given))
        low, high = pl.ds(0, part), pl.ds(part, part)
        to_pair("x low", 1, x_given.at[low], pair_x.at[low])
        to_pair("live", 0, live_half, pair_live)
        over_slots(many + part, wide, lambda slot: turn(owner(slot), slot - many, x_given))
        over_slots(0, many, lambda slot: turn(owner(slot), slot, x_kept))
    else:
        for index in range(2):
            x_kept[index * geo.wide_half : (index + 1) * geo.wide_half, :] = x_all[index].T
    for index in range(6):
        settle(("affine", index))
    gain_one, shift_one, gain_two, shift_two, gain_three, shift_three = (ref[...] for ref in affine)
    centre_one, scale_one, inverse = get_moments(0, half)
    half_one, half_two = (norm_one_half, norm_two_half) if geo.scattered else (None, None)
    activate(norm_one, half_one, slope_act_one, hidden_one, centre_one, scale_one, gain_one, shift_one)
    exchange("hidden one", 3, hidden_one.at[core], hidden_one.at[core])
    settle("middle")

    whole = slice(GUARD, GUARD + geo.rows)
    for position in range(9):
        parts[position, whole, :] = dot(
            hidden_one[core], conv_middle[span(position * geo.hidden + core * half, half), :]
        )
    settle("hidden one")
    for position in range(9):
        parts[position, whole, :] += dot(
            hidden_one[other], conv_middle[span(position * geo.hidden + other * half, half), :]
        )
    for group, value in enumerate(fold_parts(lambda position: position)):
        norm_two[geo.starts[group] : geo.starts[group] + geo.padded[group], :] = value
    send_moments(1, norm_two, half)
    if geo.scattered:
        to_pair("x high", 7, x_given.at[high], pair_x.at[high])
    for index in range(2):
        turned_one[index * half : (index + 1) * half, :] = hidden_one[index].T
    for group in range(3):
        settle(("cot", group))
        rows, real, start = geo.padded[group], geo.real[group], geo.starts[group]
        value = raw_cot[group][...].astype(F32).reshape(real, geo.wide_half)
        if rows > real:
            value = jnp.concatenate([value, jnp.zeros((rows - real, geo.wide_half), F32)], axis=0)
        cot_rows[start : start + rows, :] = value * spread(live[start : start + rows, :], geo.wide_half)
    for index in range(18):
        middle_turned[index] = conv_middle[index * half : (index + 1) * half, :].T
    centre_two, scale_two, _ = get_moments(1, half)
    activate(norm_two, half_two, slope_act_two, hidden_two, centre_two, scale_two, gain_two, shift_two)
    exchange("hidden two", 4, hidden_two.at[core], hidden_two.at[core])
    settle("last")
    norm_three[...] = dot(hidden_two[core], conv_last[span(core * half, half), :])
    settle("hidden two")
    norm_three[...] += dot(hidden_two[other], conv_last[span(other * half, half), :])
    send_moments(2, norm_three, geo.wide_half)
    if geo.scattered:
        to_pair("turned", 3, turned_one, pair_turned)
    for index in range(2):
        turned_two[index * half : (index + 1) * half, :] = hidden_two[index].T
    for index in range(2):
        last_turned[index] = conv_last[index * half : (index + 1) * half, :].T
        first_turned[index] = conv_first[index * geo.wide_half : (index + 1) * geo.wide_half, :].T
    centre_three, scale_three, inverse_wide = get_moments(2, geo.wide_half)

    def finish(rows, carry):
        grad_sum, cross_sum = carry
        normed = (norm_three[rows, :] - centre_three) * scale_three
        norm_three[rows, :] = normed
        before = normed * gain_three + shift_three + x_all[core, rows, :].astype(F32)
        share, slope = gelu_parts(before)
        out_rows[rows, :] = before * share * live_rows(rows, geo.wide_half)
        up = cot_rows[rows, :] * slope
        up_three[rows, :] = up
        return grad_sum + fold_rows(up), cross_sum + fold_rows(up * normed)

    zero_wide = jnp.zeros((8, geo.wide_half), F32)
    send_sums(3, *over_rows(finish, (zero_wide, zero_wide)))
    if geo.scattered:
        to_pair("norm two", 4, norm_two_half, pair_norm_two)
        to_pair("norm one", 2, norm_one_half, pair_norm_one)

    store_count = iter(range(15))

    def store(source, target):
        index = next(store_count)
        copy = pltpu.make_async_copy(source, target, out_sem.at[index])
        copy.start()
        pending["store", index] = copy.wait

    for group in range(3):
        start, real = geo.starts[group], geo.real[group]
        value = out_rows[start : start + real, :].reshape(geo.pixels[group], slots, geo.wide_half)
        raw_out[group][...] = value.astype(BF16)
        store(raw_out[group], outs[group])

    def slopes(up, normed, mask, target, scale, gain, sums, inverse_count, width, plain=None):
        grad_total, cross_total = sums
        factor = gain * scale
        grad_mean, cross_mean = grad_total * inverse_count, cross_total * inverse_count

        def step(rows, carry):
            gap = up[rows, :].astype(F32) - grad_mean - normed[rows, :].astype(F32) * cross_mean
            value = spread(mask[rows, :].astype(F32), width) * (factor * gap)
            if target is not None:
                target[rows, :] = value.astype(BF16)
            if plain is not None:
                plain[pl.ds(pl.multiple_of(GUARD + rows.start, CHUNK), CHUNK), :] = value
            return carry

        over_rows(step, 0)

    def give_affine(index, sums):
        affine_stage[2 * index][...] = sums[1]
        affine_stage[2 * index + 1][...] = sums[0]
        for place in (2 * index, 2 * index + 1):
            store(affine_stage[place], affine_outs[place])

    def owned(which, slot):
        if which == 2:
            return totals[2][slot]
        share = geo.shares[which]
        return totals[which][pl.ds(pl.multiple_of(owner(slot) * share, CHUNK), share), :]

    def reduced(which, slot):
        value = owned(which, slot)
        return value + recv_a[slot].astype(F32) if which == 0 else value

    quarter = wide // 4

    def rs_start(which, stage, piece, source, target, slot):
        copy = pltpu.make_async_remote_copy(
            src_ref=source,
            dst_ref=target,
            send_sem=rs_send.at[which, stage, piece],
            recv_sem=rs_recv.at[which, stage, piece],
            device_id=(owner(slot), core),
            device_id_type=MESH,
        )
        copy.start()
        pending["scatter", which, stage, piece] = copy.wait_recv
        pending["scatter sent", which, stage, piece] = copy.wait_send

    def rs_first(piece):
        low = piece * quarter

        def fill(slot):
            send_a[slot] = owned(0, slot + wide // 2).astype(BF16)

        over_slots(low, low + quarter, fill)
        part = pl.ds(low, quarter)
        rs_start(0, 0, piece, send_a.at[part], recv_a.at[part], wide // 2)

    high_slots = list(reversed(range(quarter // 2, quarter)))
    low_slots = list(reversed(range(quarter // 2)))
    far_slots = [slot for slot in high_slots + low_slots if slot]

    def rs_second(which, slots):
        send_b, recv_b = staged[which][0:2]
        for slot in slots:
            send_b[slot] = reduced(which, slot + quarter).astype(BF16)
            rs_start(which, 1, slot, send_b.at[slot], recv_b.at[slot], quarter)

    def rs_third(which, slots):
        _, recv_b, send_c, recv_c = staged[which]
        for slot in slots:
            settle(("scatter", which, 1, slot))
            send_c[slot - 1] = (reduced(which, slot) + recv_b[slot].astype(F32)).astype(BF16)
            rs_start(which, 2, slot, send_c.at[slot - 1], recv_c.at[slot - 1], slot)

    def rs_last(which):
        _, recv_b, _, recv_c = staged[which]
        settle(("scatter", which, 1, 0))
        value = reduced(which, 0) + recv_b[0].astype(F32)
        for slot in range(1, quarter):
            settle(("scatter", which, 2, slot))
            value = value + recv_c[slot - 1].astype(F32)
        weight_stage[which][...] = value
        store(weight_stage[which], weight_outs[which])

    sums_three = get_sums(3)
    slopes(
        up_three, norm_three, live, slope_three, scale_three, gain_three, sums_three, inverse_wide, geo.wide_half
    )
    send_two[...] = dot(slope_three[...], last_turned[other]).astype(BF16)
    exchange("back two", 5, send_two, recv_two)
    totals[0][...] = dot(turned_two[...], slope_three[...])
    if geo.scattered:
        rs_first(1)
    else:
        store(totals[0], weight_outs[0])
    up_two[...] = dot(slope_three[...], last_turned[core])
    give_affine(2, sums_three)
    settle("back two")

    def back_sums(up, halved, received, slope_act, normed):
        def step(rows, carry):
            value = (up[rows, :] + received[rows, :].astype(F32)) * slope_act[rows, :]
            up[rows, :] = value
            if halved is not None:
                halved[rows, :] = value.astype(BF16)
            return carry[0] + fold_rows(value), carry[1] + fold_rows(value * normed[rows, :])

        zero = jnp.zeros((8, half), F32)
        return over_rows(step, (zero, zero))

    half_up_two, half_up_one = (up_two_half, up_one_half) if geo.scattered else (None, None)
    send_sums(4, *back_sums(up_two, half_up_two, recv_two, slope_act_two, norm_two))
    if geo.scattered:
        to_pair("up two", 5, up_two_half, pair_up_two)
        rs_first(0)
        settle(("scatter", 0, 0, 1))
        rs_second(0, high_slots + low_slots)
        settle(("pair", "live"), ("pair", "norm two"), ("pair", "turned"))
    sums_two = get_sums(4)
    slopes(up_two, norm_two, live, slope_two, scale_two, gain_two, sums_two, inverse, half, shifted_src)
    if geo.scattered:
        settle(("pair", "up two"))
        slopes(
            pair_up_two, pair_norm_two, pair_live, None, scale_two, gain_two, sums_two, inverse, half, pair_src
        )

    def shift_into(source, position):
        flipped = 8 - position
        for group in range(3):
            start, rows = geo.starts[group], geo.padded[group]
            value = gather_shifted(source, flipped, group)
            if position != 4:
                value = value * spread(shift_masks[flipped, start : start + rows, :], half)
            shifted[start : start + rows, :] = value.astype(BF16)

    def back_parts(which_half):
        for position in range(9):
            parts[position, whole, :] = dot(slope_two[...], middle_turned[2 * position + which_half])
        return fold_parts(lambda position: 8 - position)

    for group, value in enumerate(back_parts(other)):
        send_one[geo.starts[group] : geo.starts[group] + geo.padded[group], :] = value.astype(BF16)
    exchange("back one", 6, send_one, recv_one)
    for position in range(9):
        place = slice(position * geo.hidden, (position + 1) * geo.hidden)
        shift_into(shifted_src, position)
        value = dot(turned_one[...], shifted[...])
        if geo.scattered:
            shift_into(pair_src, position)
            value = value + dot(pair_turned[...], shifted[...])
        totals[1][place, :] = value
    if geo.scattered:
        rs_second(1, high_slots)
        settle(("scatter", 0, 0, 0))
        rs_third(0, far_slots[:-1])
    else:
        store(totals[1], weight_outs[1])
    for group, value in enumerate(back_parts(core)):
        up_one[geo.starts[group] : geo.starts[group] + geo.padded[group], :] = value
    give_affine(1, sums_two)
    settle("back one")

    send_sums(5, *back_sums(up_one, half_up_one, recv_one, slope_act_one, norm_one))
    if geo.scattered:
        to_pair("up one", 6, up_one_half, pair_up_one)
        rs_second(1, low_slots)
        rs_third(0, far_slots[-1:])
        rs_third(1, far_slots[:-1])
        settle(("pair", "norm one"), ("pair", "x low"), ("pair", "x high"))
    sums_one = get_sums(5)
    slopes(up_one, norm_one, live, slope_one, scale_one, gain_one, sums_one, inverse, half)
    if geo.scattered:
        settle(("pair", "up one"))
        slopes(
            pair_up_one, pair_norm_one, pair_live, pair_slope, scale_one, gain_one, sums_one, inverse, half
        )
        share = geo.shares[2]
        for slot in reversed(range(wide // 2)):
            totals[2][slot] = dot(x_kept[slot], slope_one[...]) + dot(pair_x[slot], pair_slope[...])
        rs_second(2, high_slots + low_slots)
        rs_third(1, far_slots[-1:])
    else:
        totals[2][...] = dot(x_kept[...], slope_one[...])
        store(totals[2], weight_outs[2])
    send_in[...] = dot(slope_one[...], first_turned[other]).astype(BF16)
    exchange("back in", 7, send_in, recv_in)
    up_three[...] += dot(slope_one[...], first_turned[core])
    give_affine(0, sums_one)
    settle("back in")
    for group in range(3):
        start, real, rows = geo.starts[group], geo.real[group], geo.padded[group]
        value = up_three[start : start + rows, :] + recv_in[start : start + rows, :].astype(F32)
        value = value[0:real, :].reshape(geo.pixels[group], slots, geo.wide_half)
        raw_grad[group][...] = value.astype(BF16)
        store(raw_grad[group], in_grads[group])
    if geo.scattered:
        rs_third(2, far_slots)
        rs_last(0)
        rs_last(1)
        rs_last(2)
    settle_all()


def copy_kernel(count, *refs):
    sources, targets = refs[:count], refs[count : 2 * count]
    held, sem = refs[2 * count : 3 * count], refs[3 * count]
    loads = [pltpu.make_async_copy(sources[i], held[i], sem.at[0, i]) for i in range(count)]
    stores = [pltpu.make_async_copy(held[i], targets[i], sem.at[1, i]) for i in range(count)]
    for load in loads:
        load.start()
    for load, store in zip(loads, stores):
        load.wait()
        store.start()
    for store in stores:
        store.wait()


def run_block(
    wide,
    live_counts,
    small_in,
    mid_in,
    big_in,
    conv_first,
    conv_middle,
    conv_last,
    gain_first,
    shift_first,
    gain_middle,
    shift_middle,
    gain_last,
    shift_last,
    small_cot,
    mid_cot,
    big_cot,
):
    maps = (small_in, mid_in, big_in)
    cots = (small_cot, mid_cot, big_cot)
    channels = 2 * small_in.shape[3]
    hidden, half = conv_last.shape[0], conv_first.shape[1]
    geo = Geometry(wide, [tensor.shape for tensor in maps], channels, hidden, half)
    across = geo.wide_half

    def as_rows(tensor):
        count, height, width, depth = tensor.shape
        return jnp.transpose(tensor, (1, 2, 0, 3)).reshape(height * width, count, depth)

    def as_maps(rows, like):
        count, height, width, depth = like.shape
        return jnp.transpose(rows.reshape(height, width, count, depth), (2, 0, 1, 3))

    affine = [
        vector.reshape(1, -1)
        for vector in (gain_first, shift_first, gain_middle, shift_middle, gain_last, shift_last)
    ]
    operands = [
        live_counts,
        *[as_rows(tensor) for tensor in maps],
        conv_first,
        conv_middle,
        conv_last,
        *affine,
        *[as_rows(tensor) for tensor in cots],
    ]
    raw_shapes = [(count, geo.slots, across) for count in geo.pixels]
    weight_shapes = [(hidden, across), (9 * hidden, half), (channels, half)]
    share_shapes = [
        (share, shape[1]) if geo.scattered else shape
        for share, shape in zip(geo.shares, weight_shapes)
    ]
    out_shapes = [jax.ShapeDtypeStruct(shape, BF16) for shape in raw_shapes * 2]
    out_shapes += [jax.ShapeDtypeStruct(shape, F32) for shape in share_shapes]
    out_shapes += [jax.ShapeDtypeStruct(vector.shape, F32) for vector in affine]

    def vmem(dtype, *shape):
        return pltpu.VMEM(shape, dtype)

    rows, guarded = geo.rows, geo.rows + 2 * GUARD
    scratch = [vmem(BF16, *shape) for shape in raw_shapes * 4]
    scratch += [vmem(BF16, *tensor.shape) for tensor in (conv_first, conv_middle, conv_last)]
    scratch += [vmem(BF16, 2, half, across), vmem(BF16, 18, half, half), vmem(BF16, 2, across, half)]
    scratch += [vmem(F32, *vector.shape) for vector in affine]
    scratch += [vmem(F32, rows, LANES), vmem(F32, 9, rows, LANES)]
    if geo.scattered:
        x_shapes = [(wide // 2, geo.shares[2], rows)] * 2
    else:
        x_shapes = [(channels, rows), (CHUNK, LANES)]
    scratch += [vmem(BF16, 2, rows, across), *[vmem(BF16, *shape) for shape in x_shapes]]
    scratch += [vmem(F32, rows, across)]
    scratch += [vmem(F32, rows, half), vmem(F32, rows, half), vmem(F32, rows, across)]
    scratch += [vmem(F32, rows, half)] * 2
    scratch += [vmem(BF16, 2, rows, half)] * 2 + [vmem(BF16, hidden, rows)] * 2
    scratch += [vmem(F32, 9, guarded, half), vmem(F32, guarded, half), vmem(BF16, rows, half)]
    scratch += [vmem(F32, rows, across)] * 2 + [vmem(F32, rows, half)] * 2
    scratch += [vmem(BF16, rows, across), vmem(BF16, rows, half), vmem(BF16, rows, half)]
    scratch += [vmem(BF16, rows, half)] * 4 + [vmem(BF16, rows, across)] * 2
    scratch += [
        vmem(F32, wide, 3, half),
        vmem(F32, wide, 2, half),
        vmem(F32, wide, 2, across),
        vmem(F32, wide, 2, across),
        vmem(F32, wide, 2, half),
        vmem(F32, wide, 2, half),
    ]
    total_shapes = list(weight_shapes)
    if geo.scattered:
        total_shapes[2] = (wide // 2, geo.shares[2], half)
    scratch += [vmem(F32, *shape) for shape in total_shapes]
    if geo.scattered:
        scratch += [vmem(BF16, rows, half)] * 5
        scratch += [vmem(BF16, rows, LANES)] + [vmem(BF16, rows, half)] * 4
        scratch += [vmem(BF16, hidden, rows), vmem(BF16, *x_shapes[0]), vmem(F32, guarded, half)]
        scratch += [vmem(BF16, rows, LANES)]
        scratch += [vmem(BF16, wide // 2, geo.shares[0], across)] * 2
        for share, shape in zip(geo.shares, weight_shapes):
            for many in (wide // 4, wide // 4 - 1):
                scratch += [vmem(BF16, many, share, shape[1])] * 2
    scratch += [vmem(F32, *shape) for shape in (share_shapes if geo.scattered else [(8, LANES)] * 3)]
    scratch += [vmem(F32, *vector.shape) for vector in affine]
    dma = pltpu.SemaphoreType.DMA
    scratch += [dma((18,)), dma((15,)), dma((8,)), dma((8,)), dma((6,)), dma((6,))]
    if geo.scattered:
        scratch += [dma((3, 3, wide // 4))] * 2 + [dma((8,))] * 2

    anywhere = pl.BlockSpec(memory_space=pl.ANY)
    results = pl.pallas_call(
        functools.partial(block_kernel, geo),
        out_shape=out_shapes,
        in_specs=[pl.BlockSpec(memory_space=pltpu.SMEM)] + [anywhere] * (len(operands) - 1),
        out_specs=[anywhere] * len(out_shapes),
        scratch_shapes=scratch,
        compiler_params=pltpu.CompilerParams(
            collective_id=0, has_side_effects=True, vmem_limit_bytes=60 * 2**20
        ),
    )(*operands)
    results = pl.pallas_call(
        functools.partial(copy_kernel, len(results)),
        out_shape=[jax.ShapeDtypeStruct(result.shape, result.dtype) for result in results],
        in_specs=[anywhere] * len(results),
        out_specs=[anywhere] * len(results),
        scratch_shapes=[vmem(result.dtype, *result.shape) for result in results]
        + [dma((2, len(results)))],
    )(*results)
    images = [as_maps(rows, like) for rows, like in zip(results[0:6], maps * 2)]
    last_grad, middle_grad, first_grad = results[6:9]
    if not geo.scattered:
        first_grad, middle_grad, last_grad = (
            lax.psum_scatter(grad, "wide", scatter_dimension=0, tiled=True)
            for grad in (first_grad, middle_grad, last_grad)
        )
    vectors = [vector.reshape(-1) for vector in results[9:15]]
    return (*images, first_grad, middle_grad, last_grad, *vectors)


def solution(mesh):
    images = P("wide", None, None, "narrow")
    columns = P(None, "narrow")
    vector = P("narrow")
    return jax.shard_map(
        functools.partial(run_block, mesh.shape["wide"]),
        mesh=mesh,
        in_specs=(P("wide", None),) + (images,) * 3 + (columns,) * 3 + (vector,) * 6 + (images,) * 3,
        out_specs=(images,) * 6 + (P("wide", "narrow"),) * 3 + (vector,) * 6,
        check_vma=False,
    )
```
